1024 devices in a mesh: grp: 16 (over z, core), blk: 64 (over x, y).
Axes of the slice: x: 8, y: 8, z: 8, core: 2. Of those that a mesh axis runs over, the one named last changes fastest.
Arguments:
- ocean_fields: bfloat16 [40, 917504], P(None, ('grp', 'blk')), may hold values from -6 to 6
- ocean_mask: int32 [917504], P(('grp', 'blk')), may hold values 0 or 1
- entry_src: int32 [24576], P(('grp', 'blk')), may hold values from 0 to 13
- entry_route: int32 [24576, 1], P(('grp', 'blk')), may hold values from 0 to 63; in each aligned block of 24 rows (0 to 23, 24 to 47, ...) at most 2 rows name the same one
- entry_tile: int32 [24576], P(('grp', 'blk')), may hold values from 0 to 11
- weight_tiles: bfloat16 [24576, 4096], P(('grp', 'blk')), may hold values from 0 to 0.14941406
- atm_state: bfloat16 [40, 786432], P(None, ('grp', 'blk')), may hold values from -6 to 6
- atm_frac: float32 [786432], P(('grp', 'blk')), may hold values from 0 to 1
- couple: float32 [8, 40], replicated, may hold values from -1 to 1
- heat_coef: float32 [8], replicated, may hold values from -1 to 1
- kappa: float32 [30], replicated, may hold values from 0.02 to 0.15
- tracer: float32 [30, 917504], P(None, ('grp', 'blk')), may hold values from -6 to 6
- neighbours: int32 [6, 917504], P(None, ('grp', 'blk')), may hold values from 0 to 1023
Outputs:
- atm_fluxes: bfloat16 [8, 786432], P(None, ('grp', 'blk'))
- tracer_out: float32 [30, 917504], P(None, ('grp', 'blk'))
The draws below stay inside these ranges and needn't reach their ends.
Inputs may be any that keep to these rules, and one draw needn't show every extreme that they name: `entry_route`: in each aligned block of 24 rows (one device's intersection tiles) no partition is named by more than 2 rows.
All inputs are finite; a program needn't handle non-finite values. No bound on the sum of `ocean_mask` on one device may be relied on, other than what follows from the above.
Results may differ from the reference program's by a relative error of at most 0.0035.
Values may be sent and summed in bfloat16 or wider, within the bound.
No kernel may reach another device: no remote copies, remote signals or barrier semaphores. Data moves between devices by JAX's collectives and lax.ppermute only.
A program may use at most 32 MiB of HBM per device.

```python
import math
import jax
import jax.numpy as jnp
import numpy as np
from jax import lax

F = 40
NB = 8
TILE = 64
OT = 14
AT = 12
NE = 24
LEV = 30
HALO = 64
MOST = 2
OC = 896
OCEAN_CELLS = 917504
ATM_COLUMNS = 786432
ENTRIES = 24576
N_GRP = 16
N_BLK = 64


def draw_neighbours(key, part):
    key = jax.random.fold_in(key, 5)
    offsets = jax.random.randint(key, (6, OCEAN_CELLS), -HALO, HALO + 1)
    local = jnp.arange(OCEAN_CELLS, dtype=jnp.int32) % (OT * TILE)
    first = jnp.where(local == 0, -HALO, jnp.where(local == OT * TILE - 1, HALO, offsets[0]))
    offsets = offsets.at[0].set(first)
    return (local[None, :] + HALO + offsets).astype(jnp.int32)


def touch_ends(entries, own_key, least, top_value):
    place = [jax.random.randint(jax.random.fold_in(own_key, axis), (), 0, length) for axis, length in enumerate(entries.shape)]
    main_axis = entries.shape.index(max(entries.shape))
    neighbour = place[:main_axis] + [(place[main_axis] + 1) % entries.shape[main_axis]] + place[main_axis + 1:]
    return entries.at[tuple(place)].set(least).at[tuple(neighbour)].set(top_value)


def level_of(stream_key, extent, pieces, smallest, top_value):
    loudness = 1.0
    for dim, shards_of in pieces:
        steps = jax.random.uniform(jax.random.fold_in(jax.random.fold_in(stream_key, 6), dim), (shards_of,), jnp.float32, smallest / len(pieces), top_value / len(pieces))
        loudness = loudness * jnp.repeat(jnp.exp(steps), extent[dim] // shards_of).reshape((-1,) + (1,) * (len(extent) - 1 - dim))
    return loudness


def shared_out(stream_key, own, number, rows, amount, top, bound, slope):
    order = jax.random.permutation(stream_key, amount)
    crowded, ordinary = portions_of(amount, rows * top, bound, slope, True), portions_of(amount, rows * top, bound, slope, False)
    places = jnp.arange(amount)

    def named(lengths, rotation):
        used = int((lengths > 0).sum())
        fixed = max(1, used // 4)
        passed = fixed + (places - fixed + rotation * (used - fixed)) % max(1, amount - fixed)
        return jnp.zeros((amount,), jnp.int32).at[order[jnp.where(places < fixed, places, passed)]].set(jnp.asarray(lengths, jnp.int32))

    lengths = jnp.where(number % 4 == 0, named(crowded, number // 4), named(ordinary, number - number // 4 - 1))
    mixed = jax.random.permutation(jax.random.fold_in(own, 3), amount)
    source_of, receiver = mixed[0:amount // 2 * 2:2], mixed[1:amount // 2 * 2:2]
    slack = jnp.minimum(lengths[source_of] - 1, bound - lengths[receiver]) // 2
    slack = jnp.where((source_of == order[0]) | (receiver == order[0]) | (lengths[receiver] == 0), 0, jnp.maximum(slack, 0))
    passed = jax.random.randint(jax.random.fold_in(own, 4), (amount // 2,), 0, 1 << 20) % (slack + 1)
    lengths = lengths.at[source_of].add(-passed).at[receiver].add(passed)
    members = jnp.searchsorted(jnp.cumsum(lengths), jnp.arange(rows * top), side="right").astype(jnp.int32)
    table = members.reshape(top, rows).T
    table = table[jax.random.permutation(jax.random.fold_in(own, 1), rows)]
    rotation = jax.random.randint(jax.random.fold_in(own, 2), (rows, 1), 0, top)
    return jnp.take_along_axis(table, (jnp.arange(top)[None, :] + rotation) % top, axis=1)


def portions_of(number_of, total, bound, slope, full):
    weights = [(1 << 20) // math.isqrt(standing ** slope) + 1 for standing in range(1, number_of + 1)]
    largest = bound if full else min(bound, max(-(-total // number_of), total * weights[0] // sum(weights)))
    least = 1 if total - largest >= number_of - 1 else 0
    given, surplus = [largest] + [least] * (number_of - 1), total - largest - least * (number_of - 1)
    while surplus > 0:
        candidates = [i for i in range(1, number_of) if given[i] < largest] or [i for i in range(1, number_of) if given[i] < bound]
        mass, left = sum([weights[i] for i in candidates]), surplus
        for i in candidates:
            more = min(bound - given[i], max(1, left * weights[i] // mass), surplus)
            given[i] = given[i] + more
            surplus = surplus - more
    return np.array(given)


def bell_draw(rng, dims, scale, bound, cuts=(), kind=jnp.bfloat16):
    result = jax.random.normal(rng, dims, jnp.float32) * scale
    if len(cuts) > 0:
        result = level_of(rng, dims, cuts, -0.22, 0.18) * result
    return jnp.clip(result, min=-bound, max=bound).astype(kind)


def setup_inputs(seed: int = 0) -> dict:
    key_list = jax.random.split(jax.random.key(seed), 14)
    ocean_fields = bell_draw(key_list[0], (F, OCEAN_CELLS), 1.0, 6.0, ((1, 1024),))
    ocean_mask = touch_ends((jax.random.randint(key_list[1], (OCEAN_CELLS,), 0, 10) < 7).astype(jnp.int32), jax.random.fold_in(key_list[1], 1), 0, 1)
    entry_src = touch_ends(jax.random.randint(key_list[2], (ENTRIES,), 0, OT), jax.random.fold_in(key_list[2], 1), 0, OT - 1).astype(jnp.int32)
    entry_route_keys = jax.random.split(jax.random.fold_in(key_list[3], 1), ENTRIES // NE)
    entry_route_turns = jax.random.permutation(jax.random.fold_in(key_list[3], 3), ENTRIES // NE)
    entry_route = jax.vmap(lambda own, number: shared_out(jax.random.fold_in(key_list[3], 2), own, number, NE, N_BLK, 1, MOST, 2))(entry_route_keys, entry_route_turns).reshape((ENTRIES, 1))
    entry_tile = touch_ends(jax.random.randint(key_list[4], (ENTRIES,), 0, AT), jax.random.fold_in(key_list[4], 1), 0, AT - 1).astype(jnp.int32)
    weight_tiles = jnp.clip(0.14941406 * jax.random.uniform(key_list[5], (ENTRIES, TILE * TILE), jnp.float32) ** level_of(key_list[5], (ENTRIES, TILE * TILE), ((0, 1024),), -0.2, 0.2), 0.0, 0.14941406).astype(jnp.bfloat16)
    atm_state = bell_draw(key_list[6], (F, ATM_COLUMNS), 1.0, 6.0, ((1, 1024),))
    atm_frac = jnp.clip(1.0 * jax.random.uniform(key_list[7], (ATM_COLUMNS,), jnp.float32) ** level_of(key_list[7], (ATM_COLUMNS,), ((0, 1024),), -0.2, 0.2), 0.0, 1.0)
    couple = bell_draw(key_list[8], (NB, F), F ** -0.5, 1.0, (), jnp.float32)
    heat_coef = jnp.clip(jax.random.uniform(key_list[9], (NB,), jnp.float32, -1.0, 1.0), -1.0, 1.0)
    kappa = jnp.clip(jnp.exp(jax.random.uniform(key_list[10], (LEV,), jnp.float32, math.log(0.02), math.log(0.15))), 0.02, 0.15)
    tracer = bell_draw(key_list[11], (LEV, OCEAN_CELLS), 1.0, 6.0, ((1, 1024),), jnp.float32)
    neighbours = draw_neighbours(jax.random.fold_in(key_list[13], 71), 0)
    return dict(ocean_fields=ocean_fields, ocean_mask=ocean_mask, entry_src=entry_src, entry_route=entry_route, entry_tile=entry_tile, weight_tiles=weight_tiles, atm_state=atm_state, atm_frac=atm_frac, couple=couple, heat_coef=heat_coef, kappa=kappa, tracer=tracer, neighbours=neighbours)


def reference(ocean_fields, ocean_mask, entry_src, entry_route, entry_tile, weight_tiles, atm_state, atm_frac, couple, heat_coef, kappa, tracer, neighbours):
    groups = N_GRP
    peers = N_BLK
    devices = groups * peers
    mask_bf = ocean_mask.astype(jnp.bfloat16)
    masked = ocean_fields * mask_bf[None, :]
    oc_tiles = masked.reshape(F, groups, peers, OT, TILE).transpose(1, 2, 3, 0, 4).reshape(groups, peers * OT, F, TILE)
    offsets = (jnp.arange(peers, dtype=jnp.int32) * OT)[None, :, None]
    src_all = (entry_src.reshape(groups, peers, NE) + offsets).reshape(groups, peers * NE)
    dest_all = (entry_route.reshape(groups, peers, NE) * AT + entry_tile.reshape(groups, peers, NE)).reshape(groups, peers * NE)
    weights = weight_tiles.reshape(groups, peers * NE, TILE, TILE)
    state = atm_state.reshape(F, groups, peers * AT, TILE).transpose(1, 2, 0, 3)
    frac = atm_frac.reshape(groups, peers * AT, TILE)

    def one_group(items):
        fields_g, src_g, dest_g, weight_g, state_g, frac_g = items
        tiles = fields_g[src_g].astype(jnp.float32)
        wide = weight_g.astype(jnp.float32)
        contrib = jnp.einsum('efc,ecd->efd', tiles, wide).astype(jnp.bfloat16)
        remap = jax.ops.segment_sum(contrib.astype(jnp.float32), dest_g, num_segments=peers * AT)
        diff = state_g.astype(jnp.float32) - remap
        flux = jnp.einsum('bf,afd->abd', couple, diff, precision=lax.Precision.HIGHEST) * frac_g[:, None, :]
        flux = flux.astype(jnp.bfloat16)
        chosen = flux[dest_g].astype(jnp.float32)
        back = jnp.einsum('ebd,ecd->ebc', chosen, wide).astype(jnp.bfloat16)
        ocean = jax.ops.segment_sum(back.astype(jnp.float32), src_g, num_segments=peers * OT)
        return flux, ocean

    flux_all, ocean_all = lax.map(one_group, (oc_tiles, src_all, dest_all, weights, state, frac))
    atm_fluxes = flux_all.transpose(2, 0, 1, 3).reshape(NB, ATM_COLUMNS)
    mask_f = ocean_mask.astype(jnp.float32)
    ocean_flux = ocean_all.transpose(2, 0, 1, 3).reshape(NB, OCEAN_CELLS) * mask_f[None, :]
    heat = jnp.dot(heat_coef, ocean_flux, precision=lax.Precision.HIGHEST)
    heat_dev = heat.reshape(devices, OC)
    mask_dev = mask_f.reshape(devices, OC)
    near_idx = neighbours.reshape(6, devices, OC).transpose(1, 0, 2).reshape(devices, 6 * OC)
    profile = jnp.exp(-jnp.arange(LEV, dtype=jnp.float32) / 10.0)

    def one_level(items):
        level, rate, depth = items
        forced = level.reshape(devices, OC) + depth * heat_dev
        sea = forced * mask_dev
        before = jnp.roll(sea, 1, axis=0)[:, OC - HALO:]
        after = jnp.roll(sea, -1, axis=0)[:, :HALO]
        extended = jnp.concatenate([before, sea, after], axis=1)
        near = jnp.take_along_axis(extended, near_idx, axis=1).reshape(devices, 6, OC)
        spread = jnp.sum(near, axis=1) - 6.0 * forced
        return (forced + mask_dev * rate * spread).reshape(OCEAN_CELLS)

    tracer_out = lax.map(one_level, (tracer, kappa, profile))
    return atm_fluxes, tracer_out
```

```python
import jax
import jax.numpy as jnp
from jax import lax
from jax.experimental import pallas as pl
from jax.experimental.pallas import tpu as pltpu
from jax.sharding import PartitionSpec as P

TILE = 64
HALO = 64
LANES = 128
F32 = jnp.float32
BF16 = jnp.bfloat16
SMEM = pl.BlockSpec(memory_space=pltpu.SMEM)
VMEM = pl.BlockSpec(memory_space=pltpu.VMEM)


def iota(shape, dim):
    return lax.broadcasted_iota(jnp.int32, shape, dim)


def parts(value, count):
    out = []
    for _ in range(count - 1):
        high = value.astype(BF16).astype(F32)
        out.append(high)
        value = value - high
    out.append(value)
    return jnp.concatenate(out, axis=0).astype(BF16)


def column(scalars, count, rows):
    where = iota((rows, LANES), 0)
    out = jnp.zeros((rows, LANES), F32)
    for i in range(count):
        out = jnp.where(where == i, scalars[i], out)
    return out


def mm(a, b):
    return jnp.dot(a, b, preferred_element_type=F32)


def wide(col, width):
    return jnp.concatenate([col] * (width // LANES), axis=1)


def pack_kernel(src, route, tile, fields, mask, couple, weights, out, tiles, seen):
    entries = weights.shape[0]
    rows = couple.shape[0]
    for e in range(entries):
        seen[route[e]] = 0
    out[...] = jnp.zeros(out.shape, out.dtype)
    mixed = mm(parts(couple[...], 3), fields[...])
    mixed = mixed[:rows] + mixed[rows : 2 * rows] + mixed[2 * rows :]
    mixed = parts(mixed * mask[...].astype(F32), 2)
    for t in range(tiles.shape[0]):
        tiles[t] = mixed[:, t * TILE : (t + 1) * TILE]
    for e in range(entries):
        to = route[e]
        rank = seen[to]
        seen[to] = rank + 1
        sent = mm(tiles[src[e]], weights[e])
        sent = sent[:rows] + sent[rows:]
        mark = jnp.full((rows, TILE), tile[e] + 1, jnp.int32).astype(F32)
        out[to * 2 + rank] = jnp.concatenate([sent, mark], axis=1).astype(BF16)


def tables_kernel(
    src, route, near, state, frac, couple, own, edge, mixed, shares, chosen, slots, seen
):
    entries = src.shape[0]
    rows = couple.shape[0]
    cells = near.shape[1]
    for e in range(entries):
        seen[route[e]] = 0
    for e in range(entries):
        to = route[e]
        rank = seen[to]
        seen[to] = rank + 1
        slots[e] = to * 2 + rank

    part = mm(parts(couple[...], 3), state[...])
    part = part[:rows] + part[rows : 2 * rows] + part[2 * rows :]
    for t in range(state.shape[1] // TILE):
        mixed[t * rows : (t + 1) * rows, :] = part[:, t * TILE : (t + 1) * TILE]
        shares[t * rows : (t + 1) * rows, :] = jnp.broadcast_to(
            frac[:, t * TILE : (t + 1) * TILE], (rows, TILE)
        )

    low = iota((16, LANES), 1) < TILE
    for j in range(entries // 2):
        owner = jnp.where(low, src[2 * j], src[2 * j + 1])
        chosen[:, j * LANES : (j + 1) * LANES] = (iota((16, LANES), 0) == owner).astype(F32)

    def counts(place):
        total = jnp.zeros(place.shape, F32)
        for k in range(near.shape[0]):
            total = total + (near[k : k + 1, :] == place).astype(F32)
        return total.astype(BF16)

    place = iota((16, cells), 0)

    @pl.loop(0, cells // 16)
    def _(i):
        at = pl.multiple_of(i * 16, 16)
        own[pl.ds(at, 16), :] = counts(place + (at + HALO))

    @pl.loop(0, HALO // 16)
    def _(i):
        at = pl.multiple_of(i * 16, 16)
        edge[pl.ds(at, 16), :] = counts(place + at)
        edge[pl.ds(at + HALO, 16), :] = counts(place + (at + HALO + cells))


def merge_kernel(got, mixed, shares, heat_coef, fluxes, back):
    slots, rows, _ = got.shape
    peers = slots // 2
    tiles_atm = mixed.shape[0] // rows
    flat = got[...].reshape(slots * rows, LANES)
    pick = (iota((rows, LANES), 1) == TILE).astype(F32).astype(BF16)
    ids = lax.dot_general(pick, flat, (((1,), (1,)), ((), ())), preferred_element_type=F32)
    wanted = iota((peers, slots * rows), 0) * (2 * rows)
    at = iota((peers, slots * rows), 1)
    first = jnp.concatenate(
        [(at == wanted).astype(F32), (at == wanted + rows).astype(F32)], axis=0
    ).astype(BF16)
    by_slot = mm(first, flat)
    own_row = iota(ids.shape, 0) == lax.rem(iota(ids.shape, 1), rows)
    ids = jnp.where(own_row, ids, 0.0)
    member = jnp.concatenate(
        [(ids == (t + 1.0)).astype(F32) for t in range(tiles_atm)], axis=0
    ).astype(BF16)
    remap = mm(member, flat)[:, :TILE]
    flux = ((mixed[...] - remap) * shares[...]).astype(BF16)
    for t in range(tiles_atm):
        fluxes[:, t * TILE : (t + 1) * TILE] = flux[t * rows : (t + 1) * rows, :]
    coef = column(heat_coef, rows, rows)[:, :TILE]
    flux = flux.astype(F32)
    heat = [
        jnp.sum(flux[t * rows : (t + 1) * rows, :] * coef, axis=0, keepdims=True)
        for t in range(tiles_atm)
    ]
    heat = jnp.concatenate(heat + [jnp.zeros((16 - tiles_atm, TILE), F32)], axis=0)
    high = heat.astype(BF16).astype(F32)
    heat = jnp.concatenate([high, heat - high, jnp.zeros((32, TILE), F32)], axis=0)
    blank = jnp.zeros((TILE, TILE), F32)
    spread = jnp.concatenate(
        [jnp.concatenate([blank, heat], axis=1), jnp.concatenate([heat, blank], axis=1)], axis=0
    ).astype(BF16)
    lane = iota((peers, LANES), 1)
    offset = lax.rem(lane, TILE)
    target = jnp.where(offset < 32, lax.rem(lane, 16) + 1, -1).astype(F32)
    named = jnp.where(lane < TILE, pltpu.roll(by_slot[peers:], TILE, 1), by_slot[:peers])
    back[...] = mm((named == target).astype(F32).astype(BF16), spread).reshape(peers, 1, LANES)


def base_kernel(kappa, tracer, mask, own, base, edges):
    levels, cells = tracer.shape
    sea = mask[...].astype(F32)
    value = tracer[...]
    masked = value * sea
    pad = jnp.zeros((32 - levels, cells), F32)
    near = mm(parts(jnp.concatenate([masked, pad], axis=0), 2), own[...])
    near = (near[:32] + near[32:])[:levels]
    rate = wide(column(kappa, levels, levels), cells)
    base[...] = value + sea * rate * (near - 6.0 * value)
    edges[...] = jnp.concatenate([masked[:, cells - HALO :], masked[:, :HALO]], axis=1)


def profile(levels, width):
    return jnp.exp(-iota((levels, width), 0).astype(F32) / 10.0)


def heat_kernel(slots, got, chosen, flipped, mask, edges, heat, forced):
    entries = slots.shape[0]
    cells = mask.shape[1]
    low = iota((1, LANES), 1) < TILE
    pieces = []
    for j in range(entries // 2):
        one, two = slots[2 * j], slots[2 * j + 1]
        a, b = got[one // 2], got[two // 2]
        a = jnp.where(lax.rem(one, 2) == 0, a, pltpu.roll(a, TILE, 1))
        b = jnp.where(lax.rem(two, 2) == 1, b, pltpu.roll(b, TILE, 1))
        pieces.append(jnp.where(low, a, b))
    line = jnp.concatenate(pieces, axis=1)
    high = line.astype(BF16).astype(F32)
    pick = chosen[...]
    spread = jnp.concatenate([pick * high, pick * (line - high)], axis=0).astype(BF16)
    summed = mm(spread, flipped[...])
    summed = summed[:16] + summed[16:]
    row = jnp.concatenate([summed[t : t + 1, :] for t in range(cells // TILE)], axis=1)
    row = row * mask[...].astype(F32)
    heat[...] = row
    ends = jnp.concatenate([row[:, cells - HALO :], row[:, :HALO]], axis=1)
    levels = edges.shape[0]
    forced[...] = edges[...] + profile(levels, LANES) * ends


def partial_kernel(kappa, heat, own, base, mask, out):
    levels, cells = base.shape
    sea = mask[...].astype(F32)
    row = heat[...]
    high = row.astype(BF16).astype(F32)
    rows = jnp.concatenate([high, row - high, jnp.zeros((14, cells), F32)], axis=0)
    near = mm(rows.astype(BF16), own[...])
    near = near[0:1] + near[1:2]
    depth = wide(profile(levels, LANES), cells)
    rate = wide(column(kappa, levels, levels), cells)
    out[...] = base[...] + depth * (row + rate * (sea * (near - 6.0 * row)))


def finish_kernel(kappa, before, after, edge, part, mask, out):
    levels, cells = part.shape
    low = iota((levels, LANES), 1) < TILE
    halo = jnp.where(low, before[...], after[...])
    pad = jnp.zeros((32 - levels, LANES), F32)
    near = mm(parts(jnp.concatenate([halo, pad], axis=0), 2), edge[...])
    near = (near[:32] + near[32:])[:levels]
    rate = wide(column(kappa, levels, levels), cells)
    out[...] = part[...] + mask[...].astype(F32) * rate * near


def call(kernel, out_shape, in_specs, out_specs, scratch=(), flops=1_000_000):
    return pl.pallas_call(
        kernel,
        out_shape=out_shape,
        in_specs=in_specs,
        out_specs=out_specs,
        scratch_shapes=list(scratch),
        cost_estimate=pl.CostEstimate(flops=flops, bytes_accessed=2_000_000, transcendentals=0),
        compiler_params=pltpu.CompilerParams(vmem_limit_bytes=24 * 2**20),
    )


def shards(
    ocean_fields,
    ocean_mask,
    entry_src,
    entry_route,
    entry_tile,
    weight_tiles,
    atm_state,
    atm_frac,
    couple,
    heat_coef,
    kappa,
    tracer,
    neighbours,
):
    fields, cells = ocean_fields.shape
    entries = entry_src.shape[0]
    atm_cells = atm_state.shape[1]
    tiles_atm = atm_cells // TILE
    rows = couple.shape[0]
    levels = tracer.shape[0]
    peers = lax.axis_size("blk")
    shape = jax.ShapeDtypeStruct
    mask = ocean_mask.reshape(1, cells)
    route = entry_route.reshape(entries)
    weights = weight_tiles.reshape(entries, TILE, TILE)
    sent = call(
        pack_kernel,
        shape((peers * 2, rows, LANES), BF16),
        [SMEM, SMEM, SMEM, VMEM, VMEM, VMEM, VMEM],
        VMEM,
        [pltpu.VMEM((cells // TILE, 2 * rows, TILE), BF16), pltpu.SMEM((peers,), jnp.int32)],
    )(entry_src, route, entry_tile, ocean_fields, mask, couple, weights)
    got = lax.all_to_all(sent, "blk", split_axis=0, concat_axis=0, tiled=True)
    own, edge, mixed, shares, chosen, slots = call(
        tables_kernel,
        (
            shape((cells, cells), BF16),
            shape((2 * HALO, cells), BF16),
            shape((tiles_atm * rows, TILE), F32),
            shape((tiles_atm * rows, TILE), F32),
            shape((16, entries * TILE), F32),
            shape((entries,), jnp.int32),
        ),
        [SMEM, SMEM, VMEM, VMEM, VMEM, VMEM],
        (VMEM, VMEM, VMEM, VMEM, VMEM, SMEM),
        [pltpu.SMEM((peers,), jnp.int32)],
        flops=1_000_000_000,
    )(entry_src, route, neighbours, atm_state, atm_frac.reshape(1, atm_cells), couple)
    fluxes, back = call(
        merge_kernel,
        (shape((rows, atm_cells), BF16), shape((peers, 1, LANES), F32)),
        [VMEM, VMEM, VMEM, SMEM],
        (VMEM, VMEM),
    )(got, mixed, shares, heat_coef)
    returned = lax.all_to_all(back, "blk", split_axis=0, concat_axis=0, tiled=True)
    base, edges = call(
        base_kernel,
        (shape((levels, cells), F32), shape((levels, 2 * HALO), F32)),
        [SMEM, VMEM, VMEM, VMEM],
        (VMEM, VMEM),
        flops=1_000_000_000,
    )(kappa, tracer, mask, own)
    flipped = weights.transpose(0, 2, 1).reshape(entries * TILE, TILE)
    heat, forced = call(
        heat_kernel,
        (shape((1, cells), F32), shape((levels, 2 * HALO), F32)),
        [SMEM, VMEM, VMEM, VMEM, VMEM, VMEM],
        (VMEM, VMEM),
    )(slots, returned, chosen, flipped, mask, edges)
    count = lax.axis_size(("grp", "blk"))
    up = [(i, (i + 1) % count) for i in range(count)]
    down = [(target, source) for source, target in up]
    before = lax.ppermute(forced, ("grp", "blk"), up)
    after = lax.ppermute(forced, ("grp", "blk"), down)
    part = call(
        partial_kernel,
        shape((levels, cells), F32),
        [SMEM, VMEM, VMEM, VMEM, VMEM],
        VMEM,
        flops=100_000_000,
    )(kappa, heat, own, base, mask)
    tracer_out = call(
        finish_kernel,
        shape((levels, cells), F32),
        [SMEM, VMEM, VMEM, VMEM, VMEM, VMEM],
        VMEM,
    )(kappa, before, after, edge, part, mask)
    return (fluxes, tracer_out)


def solution(mesh):
    split = ("grp", "blk")
    return jax.shard_map(
        shards,
        mesh=mesh,
        in_specs=(
            P(None, split),
            P(split),
            P(split),
            P(split, None),
            P(split),
            P(split, None),
            P(None, split),
            P(split),
            P(),
            P(),
            P(),
            P(None, split),
            P(None, split),
        ),
        out_specs=(P(None, split), P(None, split)),
        check_vma=False,
    )
```

```python
import jax
import jax.numpy as jnp
from jax import lax
from jax.experimental import pallas as pl
from jax.experimental.pallas import tpu as pltpu
from jax.sharding import PartitionSpec as P

TILE = 64
HALO = 64
LANES = 128
PITCH = 33
F32 = jnp.float32
BF16 = jnp.bfloat16
SMEM = pl.BlockSpec(memory_space=pltpu.SMEM)
VMEM = pl.BlockSpec(memory_space=pltpu.VMEM)
HBM = pl.BlockSpec(memory_space=pltpu.HBM)


def iota(shape, dim):
    return lax.broadcasted_iota(jnp.int32, shape, dim)


def parts(value, count):
    out = []
    for _ in range(count - 1):
        high = value.astype(BF16).astype(F32)
        out.append(high)
        value = value - high
    out.append(value)
    return jnp.concatenate(out, axis=0).astype(BF16)


def column(scalars, count, rows):
    where = iota((rows, LANES), 0)
    out = jnp.zeros((rows, LANES), F32)
    for i in range(count):
        out = jnp.where(where == i, scalars[i], out)
    return out


def mm(a, b):
    return jnp.dot(a, b, preferred_element_type=F32)


def line(block):
    return jnp.concatenate([block[i : i + 1, :] for i in range(block.shape[0])], axis=1)


def across(col, width):
    return jnp.concatenate([col] * (width // LANES), axis=1)


def pack_kernel(
    src_hbm, route_hbm, tile_hbm, fields_hbm, mask_hbm, couple_hbm, weights_hbm, out,
    src, route, tile, fields, mask, couple, weights, tiles, wide, slots, seen, sems,
):
    pairs = (
        (fields_hbm, fields),
        (mask_hbm, mask),
        (couple_hbm, couple),
        (route_hbm, route),
        (src_hbm, src),
        (tile_hbm, tile),
        (weights_hbm, weights),
    )
    copies = [pltpu.make_async_copy(a, b, sems.at[i]) for i, (a, b) in enumerate(pairs)]
    for copy in copies:
        copy.start()
    entries = weights.shape[0]
    rows = couple.shape[0]
    half = rows // 2
    slots[...] = jnp.zeros(slots.shape, F32)
    for copy in copies[:3]:
        copy.wait()
    mixed = mm(parts(couple[...], 3), fields[...])
    mixed = mixed[:rows] + mixed[rows : 2 * rows] + mixed[2 * rows :]
    mixed = mixed * line(mask[...].astype(F32))
    high = mixed.astype(BF16).astype(F32)
    low = mixed - high
    flip = lambda x: jnp.concatenate([x[half:], x[:half]], axis=0)
    straight = jnp.concatenate([high, low], axis=0)
    swapped = jnp.concatenate([flip(high), flip(low)], axis=0)
    count = mixed.shape[1] // LANES
    stacks = [
        jnp.concatenate([x[:, j * LANES : (j + 1) * LANES] for j in range(count)], axis=0).astype(BF16)
        for x in (straight, swapped)
    ]
    for k in range(4):
        wanted = iota((LANES, TILE // 2), 1) * 2 + ((k // 2) * TILE + k % 2)
        pick = (iota((LANES, TILE // 2), 0) == wanted).astype(F32).astype(BF16)
        part = mm(stacks[k % 2], pick).astype(BF16)
        at = (k % 2) * 2 * rows
        for j in range(count):
            tiles[2 * j + k // 2, at : at + 2 * rows, :] = part[2 * rows * j : 2 * rows * (j + 1)]
    for copy in copies[3:]:
        copy.wait()
    for e in range(entries):
        seen[route[e]] = 0
    flat = weights[...].astype(F32)
    for g in range(entries // 8):
        for j in range(TILE // 2):
            wide[pl.ds(g * 8 * PITCH + j, 8, stride=PITCH), :] = flat[
                g * 8 : (g + 1) * 8, j * LANES : (j + 1) * LANES
            ]
    left = iota((rows, LANES), 1) < TILE
    for e in range(entries):
        to = route[e]
        rank = seen[to]
        seen[to] = rank + 1
        at = (to * 2 + rank) * (half + 1)
        sent = mm(tiles[src[e]], wide[e * PITCH : e * PITCH + TILE // 2, :].astype(BF16))
        even = sent[:rows] + sent[rows : 2 * rows]
        odd = sent[2 * rows : 3 * rows] + sent[3 * rows :]
        both = jnp.where(left, even, odd)
        slots[pl.ds(at, half), :] = both[:half] + pltpu.roll(both, TILE, 1)[half:]
        slots[pl.ds(at + half, 1), :] = jnp.full((1, LANES), tile[e] + 1, jnp.int32).astype(F32)
    out[...] = slots[...].astype(BF16)


def tables_kernel(
    src, route, near, state, frac, mask, couple, own, edge, mixed, shares, chosen, slots, seen
):
    entries = src.shape[0]
    rows = couple.shape[0]
    half = rows // 2
    cells = near.shape[1]
    for e in range(entries):
        seen[route[e]] = 0
    for e in range(entries):
        to = route[e]
        rank = seen[to]
        seen[to] = rank + 1
        slots[e] = to * 2 + rank

    part = mm(parts(couple[...], 3), state[...])
    part = part[:rows] + part[rows : 2 * rows] + part[2 * rows :]
    mixed[...] = jnp.zeros(mixed.shape, F32)
    shares[...] = jnp.zeros(shares.shape, F32)
    low = iota((half, LANES), 1) < TILE
    for i in range(state.shape[1] // LANES):
        here = part[:, i * LANES : (i + 1) * LANES]
        there = pltpu.roll(here, TILE, 1)
        one = jnp.where(low, here[:half], there[half:])
        two = jnp.where(low, there[:half], here[half:])
        for q in range(half):
            at = slice(q * LANES, (q + 1) * LANES)
            mixed[2 * i : 2 * i + 1, at] = one[q : q + 1]
            mixed[2 * i + 1 : 2 * i + 2, at] = two[q : q + 1]
        here = frac[i : i + 1, :]
        there = pltpu.roll(here, TILE, 1)
        shares[2 * i : 2 * i + 1, :] = jnp.where(low[:1], here, there)
        shares[2 * i + 1 : 2 * i + 2, :] = jnp.where(low[:1], there, here)

    low = iota((16, LANES), 1) < TILE
    for j in range(entries // 2):
        owner = jnp.where(low, src[2 * j], src[2 * j + 1])
        chosen[:, j * LANES : (j + 1) * LANES] = (iota((16, LANES), 0) == owner).astype(F32)

    def counts(place):
        total = jnp.zeros(place.shape, F32)
        for k in range(near.shape[0]):
            total = total + (near[k : k + 1, :] == place).astype(F32)
        return total

    place = iota((16, cells), 0)

    @pl.loop(0, cells // 16)
    def _(i):
        at = pl.multiple_of(i * 16, 16)
        own[pl.ds(at, 16), :] = counts(place + (at + HALO)).astype(BF16)

    sea = line(mask[...].astype(F32))

    @pl.loop(0, HALO // 16)
    def _(i):
        at = pl.multiple_of(i * 16, 16)
        edge[pl.ds(at, 16), :] = (sea * counts(place + at)).astype(BF16)
        edge[pl.ds(at + HALO, 16), :] = (sea * counts(place + (at + HALO + cells))).astype(BF16)


def merge_kernel(heat_coef, got, mixed, shares, fluxes, back, flat):
    half = mixed.shape[1] // LANES
    peers = back.shape[0]
    pitch = 2 * (half + 1)
    flat[...] = got[...].astype(F32)
    row = lambda rank, q: flat[pl.ds(rank * (half + 1) + q, peers, stride=pitch), :]
    first, second = row(0, half), row(1, half)
    named = jnp.concatenate([first, second], axis=0).astype(BF16)
    pick = (iota((16, LANES), 1) == 0).astype(F32).astype(BF16)
    ids = lax.dot_general(pick, named, (((1,), (1,)), ((), ())), preferred_element_type=F32)
    member = (ids == (iota(ids.shape, 0) + 1).astype(F32)).astype(F32).astype(BF16)
    values = jnp.concatenate(
        [jnp.concatenate([row(0, q), row(1, q)], axis=0) for q in range(half)], axis=1
    ).astype(BF16)
    remap = mm(member, values)
    low = iota((1, LANES), 1) < TILE
    heat = jnp.zeros((16, LANES), F32)
    for q in range(half):
        at = slice(q * LANES, (q + 1) * LANES)
        flux = ((mixed[:, at] - remap[:, at]) * shares[...]).astype(BF16).astype(F32)
        fluxes[:, at] = flux
        heat = heat + flux * jnp.where(low, heat_coef[q], heat_coef[q + half])
    heat = heat + pltpu.roll(heat, TILE, 1)
    high = heat.astype(BF16).astype(F32)
    heat = jnp.concatenate([high, heat - high], axis=0)
    blank = jnp.zeros((32, LANES), F32)
    spread = jnp.concatenate(
        [jnp.where(low, heat, 0.0), blank, jnp.where(low, 0.0, heat), blank], axis=0
    ).astype(BF16)
    lane = iota((peers, LANES), 1)
    target = jnp.where((lane & (TILE - 1)) < 32, (lane & 15) + 1, -1).astype(F32)
    asked = jnp.where(lane < TILE, first, second)
    back[...] = mm((asked == target).astype(F32).astype(BF16), spread).reshape(back.shape)


def base_kernel(kappa, tracer, mask, own, base, edges, depth, rate):
    levels, cells = tracer.shape
    sea = line(mask[...].astype(F32))
    value = tracer[...]
    masked = value * sea
    pad = jnp.zeros((32 - levels, cells), F32)
    near = mm(parts(jnp.concatenate([masked, pad], axis=0), 2), own[...])
    near = (near[:32] + near[32:])[:levels]
    speed = column(kappa, levels, levels)
    rate[...] = speed
    depth[...] = jnp.exp(-iota((levels, LANES), 0).astype(F32) / 10.0)
    base[...] = value + sea * (across(speed, cells) * (near - 6.0 * value))
    edges[...] = jnp.concatenate([masked[:, cells - HALO :], masked[:, :HALO]], axis=1)


def heat_kernel(slots, got, chosen, flipped, mask, edges, depth, heat, forced):
    entries = slots.shape[0]
    cells = heat.shape[1]
    low = iota((1, LANES), 1) < TILE
    pieces = []
    for j in range(entries // 2):
        one, two = slots[2 * j], slots[2 * j + 1]
        a, b = got[one >> 1], got[two >> 1]
        a = jnp.where((one & 1) == 0, a, pltpu.roll(a, TILE, 1))
        b = jnp.where((two & 1) == 1, b, pltpu.roll(b, TILE, 1))
        pieces.append(jnp.where(low, a, b))
    found = jnp.concatenate(pieces, axis=1)
    high = found.astype(BF16).astype(F32)
    pick = chosen[...]
    spread = jnp.concatenate([pick * high, pick * (found - high)], axis=0).astype(BF16)
    summed = mm(spread, flipped[...])
    summed = summed[:16] + summed[16:]
    row = jnp.concatenate([summed[t : t + 1, :] for t in range(cells // TILE)], axis=1)
    row = row * line(mask[...].astype(F32))
    heat[...] = row
    ends = jnp.concatenate([row[:, cells - HALO :], row[:, :HALO]], axis=1)
    forced[...] = edges[...] + depth[...] * ends


def partial_kernel(heat, own, base, mask, depth, rate, fluxes, out, placed):
    half = placed.shape[0] // 2
    low = iota((half, LANES), 1) < TILE
    for i in range(placed.shape[1] // LANES):
        piece = lambda t: jnp.concatenate(
            [fluxes[t : t + 1, q * LANES : (q + 1) * LANES] for q in range(half)], axis=0
        )
        one, two = piece(2 * i), piece(2 * i + 1)
        block = jnp.concatenate(
            [
                jnp.where(low, one, pltpu.roll(two, TILE, 1)),
                jnp.where(low, pltpu.roll(one, TILE, 1), two),
            ],
            axis=0,
        )
        placed[:, i * LANES : (i + 1) * LANES] = block.astype(BF16)
    levels, cells = base.shape
    sea = line(mask[...].astype(F32))
    row = heat[...]
    high = row.astype(BF16).astype(F32)
    rows = jnp.concatenate([high, row - high, jnp.zeros((14, cells), F32)], axis=0)
    near = mm(rows.astype(BF16), own[...])
    near = sea * (near[0:1] + near[1:2] - 6.0 * row)
    out[...] = base[...] + across(depth[...], cells) * (row + across(rate[...], cells) * near)


def finish_kernel(before, after, edge, part, rate, out):
    levels = part.shape[0]
    low = iota((levels, LANES), 1) < TILE
    halo = jnp.where(low, before[...], after[...]) * rate[...]
    pad = jnp.zeros((32 - levels, LANES), F32)
    near = mm(parts(jnp.concatenate([halo, pad], axis=0), 2), edge[...])
    out[...] = part[...] + (near[:32] + near[32:])[:levels]


def call(kernel, out_shape, in_specs, out_specs, scratch=(), flops=1_000_000, vmem=24 * 2**20):
    return pl.pallas_call(
        kernel,
        out_shape=out_shape,
        in_specs=in_specs,
        out_specs=out_specs,
        scratch_shapes=list(scratch),
        cost_estimate=pl.CostEstimate(flops=flops, bytes_accessed=2_000_000, transcendentals=0),
        compiler_params=pltpu.CompilerParams(vmem_limit_bytes=vmem),
    )


def shards(
    ocean_fields,
    ocean_mask,
    entry_src,
    entry_route,
    entry_tile,
    weight_tiles,
    atm_state,
    atm_frac,
    couple,
    heat_coef,
    kappa,
    tracer,
    neighbours,
):
    fields, cells = ocean_fields.shape
    entries = entry_src.shape[0]
    atm_cells = atm_state.shape[1]
    rows = couple.shape[0]
    levels = tracer.shape[0]
    peers = lax.axis_size("blk")
    shape = jax.ShapeDtypeStruct
    half = rows // 2
    mask = ocean_mask.reshape(cells // LANES, LANES)
    route = entry_route.reshape(entries)
    pitch = 2 * (half + 1)
    i32 = jnp.int32
    sent = call(
        pack_kernel,
        shape((peers * pitch, LANES), BF16),
        [HBM] * 7,
        VMEM,
        [
            pltpu.SMEM((entries,), i32),
            pltpu.SMEM((entries,), i32),
            pltpu.SMEM((entries,), i32),
            pltpu.VMEM((fields, cells), BF16),
            pltpu.VMEM((cells // LANES, LANES), i32),
            pltpu.VMEM((rows, fields), F32),
            pltpu.VMEM((entries, TILE * TILE), BF16),
            pltpu.VMEM((cells // TILE, 4 * rows, TILE // 2), BF16),
            pltpu.VMEM((entries * PITCH, LANES), F32),
            pltpu.VMEM((peers * pitch, LANES), F32),
            pltpu.SMEM((peers,), i32),
            pltpu.SemaphoreType.DMA((7,)),
        ],
        vmem=64 * 2**20,
    )(entry_src, route, entry_tile, ocean_fields, mask, couple, weight_tiles)
    sent, weight_tiles, neighbours, atm_state = lax.optimization_barrier(
        (sent, weight_tiles, neighbours, atm_state)
    )
    got = lax.all_to_all(
        sent.reshape(peers, half + 1, 2, LANES), "blk", split_axis=0, concat_axis=0, tiled=True
    ).reshape(peers * pitch, LANES)
    own, edge, mixed, shares, chosen, slots = call(
        tables_kernel,
        (
            shape((cells, cells), BF16),
            shape((2 * HALO, cells), BF16),
            shape((16, half * LANES), F32),
            shape((16, LANES), F32),
            shape((16, entries * TILE), F32),
            shape((entries,), i32),
        ),
        [SMEM, SMEM, VMEM, VMEM, VMEM, VMEM, VMEM],
        (VMEM, VMEM, VMEM, VMEM, VMEM, SMEM),
        [pltpu.SMEM((peers,), i32)],
        flops=1_000_000_000,
    )(
        entry_src,
        route,
        neighbours,
        atm_state,
        atm_frac.reshape(atm_cells // LANES, LANES),
        mask,
        couple,
    )
    base, edges, depth, rate = call(
        base_kernel,
        (
            shape((levels, cells), F32),
            shape((levels, 2 * HALO), F32),
            shape((levels, LANES), F32),
            shape((levels, LANES), F32),
        ),
        [SMEM, VMEM, VMEM, VMEM],
        (VMEM,) * 4,
        flops=1_000_000_000,
    )(kappa, tracer, mask, own)
    flipped = weight_tiles.reshape(entries, TILE, TILE).transpose(0, 2, 1)
    flipped = flipped.reshape(entries * TILE, TILE)
    got, mixed, base, edges, flipped, own = lax.optimization_barrier(
        (got, mixed, base, edges, flipped, own)
    )
    fluxes, back = call(
        merge_kernel,
        (shape((16, half * LANES), F32), shape((peers, 1, LANES), F32)),
        [SMEM, VMEM, VMEM, VMEM],
        (VMEM, VMEM),
        [pltpu.VMEM((peers * pitch, LANES), F32)],
    )(heat_coef, got, mixed, shares)
    returned = lax.all_to_all(back, "blk", split_axis=0, concat_axis=0, tiled=True)
    heat, forced = call(
        heat_kernel,
        (shape((1, cells), F32), shape((levels, 2 * HALO), F32)),
        [SMEM] + [VMEM] * 6,
        (VMEM, VMEM),
    )(slots, returned, chosen, flipped, mask, edges, depth)
    count = lax.axis_size(("grp", "blk"))
    up = [(i, (i + 1) % count) for i in range(count)]
    down = [(target, source) for source, target in up]
    before = lax.ppermute(forced, ("grp", "blk"), up)
    after = lax.ppermute(forced, ("grp", "blk"), down)
    part, fluxes = call(
        partial_kernel,
        (shape((levels, cells), F32), shape((rows, atm_cells), BF16)),
        [VMEM] * 7,
        (VMEM, VMEM),
        flops=100_000_000,
    )(heat, own, base, mask, depth, rate, fluxes)
    tracer_out = call(finish_kernel, shape((levels, cells), F32), [VMEM] * 5, VMEM)(
        before, after, edge, part, rate
    )
    return (fluxes, tracer_out)


def solution(mesh):
    split = ("grp", "blk")
    return jax.shard_map(
        shards,
        mesh=mesh,
        in_specs=(
            P(None, split),
            P(split),
            P(split),
            P(split, None),
            P(split),
            P(split, None),
            P(None, split),
            P(split),
            P(),
            P(),
            P(),
            P(None, split),
            P(None, split),
        ),
        out_specs=(P(None, split), P(None, split)),
        check_vma=False,
    )
```

```python
import jax
import jax.numpy as jnp
from jax import lax
from jax.experimental import pallas as pl
from jax.experimental.pallas import tpu as pltpu
from jax.sharding import PartitionSpec as P

TILE = 64
HALO = 64
LANES = 128
PITCH = 33
F32 = jnp.float32
BF16 = jnp.bfloat16
SMEM = pl.BlockSpec(memory_space=pltpu.SMEM)
VMEM = pl.BlockSpec(memory_space=pltpu.VMEM)
HBM = pl.BlockSpec(memory_space=pltpu.HBM)


def iota(shape, dim):
    return lax.broadcasted_iota(jnp.int32, shape, dim)


def parts(value, count):
    out = []
    for _ in range(count - 1):
        high = value.astype(BF16).astype(F32)
        out.append(high)
        value = value - high
    out.append(value)
    return jnp.concatenate(out, axis=0).astype(BF16)


def column(scalars, count, rows):
    where = iota((rows, LANES), 0)
    out = jnp.zeros((rows, LANES), F32)
    for i in range(count):
        out = jnp.where(where == i, scalars[i], out)
    return out


def mm(a, b):
    return jnp.dot(a, b, preferred_element_type=F32)


def line(block):
    return jnp.concatenate([block[i : i + 1, :] for i in range(block.shape[0])], axis=1)


def across(col, width):
    return jnp.concatenate([col] * (width // LANES), axis=1)


def pack_kernel(
    src_hbm, route_hbm, tile_hbm, fields_hbm, mask_hbm, couple_hbm, weights_hbm, out,
    src, route, tile, fields, mask, couple, weights, tiles, wide, slots, seen, sems,
):
    pairs = (
        (fields_hbm, fields),
        (mask_hbm, mask),
        (couple_hbm, couple),
        (route_hbm, route),
        (src_hbm, src),
        (tile_hbm, tile),
        (weights_hbm, weights),
    )
    copies = [pltpu.make_async_copy(a, b, sems.at[i]) for i, (a, b) in enumerate(pairs)]
    for copy in copies:
        copy.start()
    entries = weights.shape[0]
    rows = couple.shape[0]
    half = rows // 2
    slots[...] = jnp.zeros(slots.shape, F32)
    for copy in copies[:3]:
        copy.wait()
    mixed = mm(parts(couple[...], 3), fields[...])
    mixed = mixed[:rows] + mixed[rows : 2 * rows] + mixed[2 * rows :]
    mixed = mixed * line(mask[...].astype(F32))
    high = mixed.astype(BF16).astype(F32)
    low = mixed - high
    flip = lambda x: jnp.concatenate([x[half:], x[:half]], axis=0)
    straight = jnp.concatenate([high, low], axis=0)
    swapped = jnp.concatenate([flip(high), flip(low)], axis=0)
    count = mixed.shape[1] // LANES
    stacks = [
        jnp.concatenate([x[:, j * LANES : (j + 1) * LANES] for j in range(count)], axis=0).astype(BF16)
        for x in (straight, swapped)
    ]
    for k in range(4):
        wanted = iota((LANES, TILE // 2), 1) * 2 + ((k // 2) * TILE + k % 2)
        pick = (iota((LANES, TILE // 2), 0) == wanted).astype(F32).astype(BF16)
        part = mm(stacks[k % 2], pick).astype(BF16)
        at = (k % 2) * 2 * rows
        for j in range(count):
            tiles[2 * j + k // 2, at : at + 2 * rows, :] = part[2 * rows * j : 2 * rows * (j + 1)]
    for copy in copies[3:]:
        copy.wait()
    for e in range(entries):
        seen[route[e]] = 0
    flat = weights[...].astype(F32)
    for g in range(entries // 8):
        for j in range(TILE // 2):
            wide[pl.ds(g * 8 * PITCH + j, 8, stride=PITCH), :] = flat[
                g * 8 : (g + 1) * 8, j * LANES : (j + 1) * LANES
            ]
    left = iota((rows, LANES), 1) < TILE
    for e in range(entries):
        to = route[e]
        rank = seen[to]
        seen[to] = rank + 1
        at = (to * 2 + rank) * (half + 1)
        sent = mm(tiles[src[e]], wide[e * PITCH : e * PITCH + TILE // 2, :].astype(BF16))
        even = sent[:rows] + sent[rows : 2 * rows]
        odd = sent[2 * rows : 3 * rows] + sent[3 * rows :]
        both = jnp.where(left, even, odd)
        slots[pl.ds(at, half), :] = both[:half] + pltpu.roll(both, TILE, 1)[half:]
        slots[pl.ds(at + half, 1), :] = jnp.full((1, LANES), tile[e] + 1, jnp.int32).astype(F32)
    out[...] = slots[...].astype(BF16)


def ship_kernel(src, route, flipped, tracer, mask, out, seen):
    entries = src.shape[0]
    levels, cells = tracer.shape
    half = entries * TILE // 2
    for e in range(entries):
        seen[route[e]] = 0
    slots = []
    for e in range(entries):
        to = route[e]
        rank = seen[to]
        seen[to] = rank + 1
        slots.append(to * 2 + rank)
    out[:half, :] = jnp.concatenate([flipped[:half, :], flipped[half:, :]], axis=1)
    ends = lambda x: jnp.concatenate([x[:, cells - HALO :], x[:, :HALO]], axis=1)
    sea = ends(line(mask[...].astype(F32)))
    edge = ends(tracer[...]) * sea
    out[half : half + 32, :] = jnp.concatenate(
        [edge, jnp.broadcast_to(sea, (32 - levels, LANES))], axis=0
    ).astype(BF16)
    where = iota((32, LANES), 0)
    slot_rows = jnp.full((32, LANES), -1, jnp.int32)
    tile_rows = jnp.full((32, LANES), -1, jnp.int32)
    for e in range(entries):
        here = where == (e // 2 + 16 * (e % 2))
        slot_rows = jnp.where(here, slots[e], slot_rows)
        tile_rows = jnp.where(here, src[e], tile_rows)
    out[half + 32 : half + 64, :] = slot_rows.astype(F32).astype(BF16)
    out[half + 64 : half + 96, :] = tile_rows.astype(F32).astype(BF16)


def tables_kernel(src, state, frac, couple, mixed, shares, chosen):
    entries = src.shape[0]
    rows = couple.shape[0]
    half = rows // 2
    part = mm(parts(couple[...], 3), state[...])
    part = part[:rows] + part[rows : 2 * rows] + part[2 * rows :]
    mixed[...] = jnp.zeros(mixed.shape, F32)
    shares[...] = jnp.zeros(shares.shape, F32)
    low = iota((half, LANES), 1) < TILE
    for i in range(state.shape[1] // LANES):
        here = part[:, i * LANES : (i + 1) * LANES]
        there = pltpu.roll(here, TILE, 1)
        one = jnp.where(low, here[:half], there[half:])
        two = jnp.where(low, there[:half], here[half:])
        for q in range(half):
            at = slice(q * LANES, (q + 1) * LANES)
            mixed[2 * i : 2 * i + 1, at] = one[q : q + 1]
            mixed[2 * i + 1 : 2 * i + 2, at] = two[q : q + 1]
        here = frac[i : i + 1, :]
        there = pltpu.roll(here, TILE, 1)
        shares[2 * i : 2 * i + 1, :] = jnp.where(low[:1], here, there)
        shares[2 * i + 1 : 2 * i + 2, :] = jnp.where(low[:1], there, here)

    low = iota((16, LANES), 1) < TILE
    for j in range(entries // 2):
        owner = jnp.where(low, src[2 * j], src[2 * j + 1])
        chosen[:, j * LANES : (j + 1) * LANES] = (iota((16, LANES), 0) == owner).astype(F32)


def merge_kernel(heat_coef, got, mixed, shares, fluxes, back, flat):
    half = mixed.shape[1] // LANES
    peers = back.shape[0] // 4
    pitch = 2 * (half + 1)
    flat[...] = got[...].astype(F32)
    row = lambda rank, q: flat[pl.ds(rank * (half + 1) + q, peers, stride=pitch), :]
    first, second = row(0, half), row(1, half)
    named = jnp.concatenate([first, second], axis=0).astype(BF16)
    pick = (iota((16, LANES), 1) == 0).astype(F32).astype(BF16)
    ids = lax.dot_general(pick, named, (((1,), (1,)), ((), ())), preferred_element_type=F32)
    member = (ids == (iota(ids.shape, 0) + 1).astype(F32)).astype(F32).astype(BF16)
    values = jnp.concatenate(
        [jnp.concatenate([row(0, q), row(1, q)], axis=0) for q in range(half)], axis=1
    ).astype(BF16)
    remap = mm(member, values)
    low = iota((1, LANES), 1) < TILE
    heat = jnp.zeros((16, LANES), F32)
    for q in range(half):
        at = slice(q * LANES, (q + 1) * LANES)
        flux = ((mixed[:, at] - remap[:, at]) * shares[...]).astype(BF16).astype(F32)
        fluxes[:, at] = flux
        heat = heat + flux * jnp.where(low, heat_coef[q], heat_coef[q + half])
    heat = heat + pltpu.roll(heat, TILE, 1)
    high = heat.astype(BF16).astype(F32)
    heat = jnp.concatenate([high, heat - high], axis=0)
    blank = jnp.zeros((32, LANES), F32)
    spread = jnp.concatenate(
        [jnp.where(low, heat, 0.0), blank, jnp.where(low, 0.0, heat), blank], axis=0
    ).astype(BF16)
    lane = iota((peers, LANES), 1)
    target = jnp.where((lane & (TILE - 1)) < 32, (lane & 15) + 1, -1).astype(F32)
    asked = jnp.where(lane < TILE, first, second)
    reply = mm((asked == target).astype(F32).astype(BF16), spread)
    high = reply.astype(BF16).astype(F32)
    four = (high, reply - high, pltpu.roll(high, 1, 0), pltpu.roll(high, peers - 1, 0))
    for k, rows in enumerate(four):
        flat[pl.ds(k, peers, stride=4), :] = rows
    back[...] = flat[: 4 * peers, :].astype(BF16)


def base_kernel(kappa, near, tracer, mask, own, edge, base, depth, speed, rate):
    levels, cells = tracer.shape
    place = iota((LANES, cells), 0).astype(F32).astype(BF16)

    def counts(start):
        total = jnp.zeros(place.shape, BF16)
        for k in range(near.shape[0]):
            at = jnp.clip(near[k : k + 1, :] - start, -1, LANES).astype(F32).astype(BF16)
            total = total + jnp.where(at == place, jnp.ones((), BF16), jnp.zeros((), BF16))
        return total

    @pl.loop(0, cells // LANES)
    def _(i):
        at = pl.multiple_of(i * LANES, LANES)
        own[pl.ds(at, LANES), :] = counts(at + HALO)

    sea = line(mask[...].astype(F32))
    land = sea.astype(BF16)
    edge[:HALO, :] = (land * counts(0))[:HALO]
    edge[HALO:, :] = (land * counts(cells + HALO))[:HALO]

    value = tracer[...]
    pad = jnp.zeros((32 - levels, cells), F32)
    total = mm(parts(jnp.concatenate([value * sea, pad], axis=0), 2), own[...])
    total = sea * ((total[:32] + total[32:])[:levels] - 6.0 * value)
    pace = column(kappa, levels, levels)
    deep = jnp.exp(-iota((levels, LANES), 0).astype(F32) / 10.0)
    depth[...] = deep
    speed[...] = pace
    rate[...] = deep * pace
    base[...] = value + across(pace, cells) * total


def in_group(shape):
    me = lax.axis_index("blk")
    low = iota(shape, 1) < TILE
    return jnp.where(low, me, lax.axis_size("blk") - 1 - me) > 0


def heat_kernel(got, chosen, here, before, after, mask, depth, heat, forced, halo, flat):
    cells = heat.shape[1]
    half = here.shape[0] - 96
    lane = iota((32, LANES), 1)
    target = ((lane & (TILE - 1)) * 2 + (lane >> 6)).astype(F32)
    meta = lambda ref, at: ref[half + at : half + at + 32, :].astype(F32)
    found = lambda ref: meta(ref, 32) == target
    last = float(cells // TILE - 1)
    picks = [
        pick.astype(F32).astype(BF16)
        for pick in (
            found(here),
            found(before) & (meta(before, 64) == last),
            found(after) & (meta(after, 64) == 0.0),
        )
    ]
    peers = got.shape[0] // 4
    count = half // LANES
    flat[...] = got[...].astype(F32)
    low = iota((16, LANES), 1) < TILE

    def lookup(k, which):
        rows = flat[pl.ds(k, peers, stride=4), :]
        turned = pltpu.roll(rows, TILE, 1)
        one = jnp.concatenate([rows, turned], axis=0).astype(BF16)
        two = jnp.concatenate([turned, rows], axis=0).astype(BF16)
        return jnp.where(low, mm(picks[which][:16], one), mm(picks[which][16:], two))

    def laid(rows, start):
        return jnp.concatenate([rows[j : j + 1] for j in range(start, start + count)], axis=1)

    high, rest = lookup(0, 0), lookup(1, 0)
    previous, following = lookup(2, 1), lookup(3, 2)
    spread = []
    for h in range(2):
        pick = chosen[:, h * half : (h + 1) * half]
        for rows in (high, rest):
            spread.append(pick * laid(rows, h * count))
    summed = mm(jnp.concatenate(spread, axis=0).astype(BF16), here[:half, :])
    summed = summed[:16] + summed[16:32] + pltpu.roll(summed[32:48] + summed[48:], TILE, 1)
    blank = jnp.zeros((14, half), F32)

    def side(rows, ref):
        rows = jnp.concatenate([laid(rows, 0), laid(rows, count), blank], axis=0)
        return mm(rows.astype(BF16), ref[:half, :])

    left, right = side(previous, before), side(following, after)
    left = left[0:1] + pltpu.roll(left, TILE, 1)[1:2]
    right = right[1:2] + pltpu.roll(right, TILE, 1)[0:1]
    levels = depth.shape[0]
    coast = jnp.where(low[:1], meta(before, 0)[levels : levels + 1], meta(after, 0)[levels : levels + 1])
    halo[...] = jnp.where(low[:1], left, right) * coast
    row = jnp.concatenate([summed[t : t + 1, :TILE] for t in range(cells // TILE)], axis=1)
    row = row * line(mask[...].astype(F32))
    heat[...] = row
    ends = jnp.concatenate([row[:, cells - HALO :], row[:, :HALO]], axis=1)
    forced[...] = meta(here, 0)[:levels] + depth[...] * ends


def halves(row):
    high = row.astype(BF16).astype(F32)
    blank = jnp.zeros((14, row.shape[1]), F32)
    return jnp.concatenate([high, row - high, blank], axis=0).astype(BF16)


def partial_kernel(heat, own, base, mask, depth, rate, fluxes, out, placed):
    half = placed.shape[0] // 2
    low = iota((half, LANES), 1) < TILE
    for i in range(placed.shape[1] // LANES):
        piece = lambda t: jnp.concatenate(
            [fluxes[t : t + 1, q * LANES : (q + 1) * LANES] for q in range(half)], axis=0
        )
        one, two = piece(2 * i), piece(2 * i + 1)
        block = jnp.concatenate(
            [
                jnp.where(low, one, pltpu.roll(two, TILE, 1)),
                jnp.where(low, pltpu.roll(one, TILE, 1), two),
            ],
            axis=0,
        )
        placed[:, i * LANES : (i + 1) * LANES] = block.astype(BF16)
    cells = base.shape[1]
    sea = line(mask[...].astype(F32))
    row = heat[...]
    near = mm(halves(row), own[...])
    near = sea * (near[0:1] + near[1:2] - 6.0 * row)
    out[...] = base[...] + across(depth[...], cells) * row + across(rate[...], cells) * near


def finish_kernel(halo, swapped, before, after, edge, part, speed, rate, out):
    levels, cells = part.shape
    first = before.shape[0] - 96
    rows = slice(first, first + 32)
    low = iota((32, LANES), 1) < TILE
    outer = jnp.where(low, before[rows, :].astype(F32), after[rows, :].astype(F32))[:levels]
    outer = jnp.where(in_group((levels, LANES)), outer, swapped[...]) * speed[...]
    pad = jnp.zeros((32 - levels, LANES), F32)
    outer = parts(jnp.concatenate([outer, pad], axis=0), 2)
    inner = halves(jnp.where(in_group((1, LANES)), halo[...], 0.0))
    near = mm(jnp.concatenate([outer, inner], axis=0), edge[...])
    inner = near[64:65] + near[65:66]
    out[...] = part[...] + (near[:32] + near[32:64])[:levels] + across(rate[...], cells) * inner


def call(kernel, out_shape, in_specs, out_specs, scratch=(), flops=1_000_000, vmem=24 * 2**20):
    return pl.pallas_call(
        kernel,
        out_shape=out_shape,
        in_specs=in_specs,
        out_specs=out_specs,
        scratch_shapes=list(scratch),
        cost_estimate=pl.CostEstimate(flops=flops, bytes_accessed=2_000_000, transcendentals=0),
        compiler_params=pltpu.CompilerParams(vmem_limit_bytes=vmem),
    )


def shards(
    ocean_fields,
    ocean_mask,
    entry_src,
    entry_route,
    entry_tile,
    weight_tiles,
    atm_state,
    atm_frac,
    couple,
    heat_coef,
    kappa,
    tracer,
    neighbours,
):
    fields, cells = ocean_fields.shape
    entries = entry_src.shape[0]
    atm_cells = atm_state.shape[1]
    rows = couple.shape[0]
    levels = tracer.shape[0]
    peers = lax.axis_size("blk")
    shape = jax.ShapeDtypeStruct
    half = rows // 2
    mask = ocean_mask.reshape(cells // LANES, LANES)
    route = entry_route.reshape(entries)
    pitch = 2 * (half + 1)
    i32 = jnp.int32
    sent = call(
        pack_kernel,
        shape((peers * pitch, LANES), BF16),
        [HBM] * 7,
        VMEM,
        [
            pltpu.SMEM((entries,), i32),
            pltpu.SMEM((entries,), i32),
            pltpu.SMEM((entries,), i32),
            pltpu.VMEM((fields, cells), BF16),
            pltpu.VMEM((cells // LANES, LANES), i32),
            pltpu.VMEM((rows, fields), F32),
            pltpu.VMEM((entries, TILE * TILE), BF16),
            pltpu.VMEM((cells // TILE, 4 * rows, TILE // 2), BF16),
            pltpu.VMEM((entries * PITCH, LANES), F32),
            pltpu.VMEM((peers * pitch, LANES), F32),
            pltpu.SMEM((peers,), i32),
            pltpu.SemaphoreType.DMA((7,)),
        ],
        vmem=64 * 2**20,
    )(entry_src, route, entry_tile, ocean_fields, mask, couple, weight_tiles)
    sent, weight_tiles, neighbours, atm_state, tracer = lax.optimization_barrier(
        (sent, weight_tiles, neighbours, atm_state, tracer)
    )
    got = lax.all_to_all(
        sent.reshape(peers, half + 1, 2, LANES), "blk", split_axis=0, concat_axis=0, tiled=True
    ).reshape(peers * pitch, LANES)
    flipped = weight_tiles.reshape(entries, TILE, TILE).transpose(0, 2, 1)
    here = call(
        ship_kernel,
        shape((entries * TILE // 2 + 96, LANES), BF16),
        [SMEM, SMEM, VMEM, VMEM, VMEM],
        VMEM,
        [pltpu.SMEM((peers,), i32)],
    )(entry_src, route, flipped.reshape(entries * TILE, TILE), tracer, mask)
    axes = ("grp", "blk")
    count = lax.axis_size(axes)
    ring = [(i, (i + 1) % count) for i in range(count)]
    up = [pair for pair in ring if pair[1] % peers]
    seams = [pair for pair in ring if pair[1] % peers == 0]
    down = [(target, source) for source, target in up]
    before = lax.ppermute(here, axes, up)
    after = lax.ppermute(here, axes, down)
    mixed, shares, chosen = call(
        tables_kernel,
        (
            shape((16, half * LANES), F32),
            shape((16, LANES), F32),
            shape((16, entries * TILE), F32),
        ),
        [SMEM, VMEM, VMEM, VMEM],
        (VMEM,) * 3,
    )(entry_src, atm_state, atm_frac.reshape(atm_cells // LANES, LANES), couple)
    fluxes, back = call(
        merge_kernel,
        (shape((16, half * LANES), F32), shape((peers * 4, LANES), BF16)),
        [SMEM, VMEM, VMEM, VMEM],
        (VMEM, VMEM),
        [pltpu.VMEM((peers * pitch, LANES), F32)],
    )(heat_coef, got, mixed, shares)
    back, neighbours, tracer = lax.optimization_barrier((back, neighbours, tracer))
    returned = lax.all_to_all(
        back.reshape(peers, 2, 2, LANES), "blk", split_axis=0, concat_axis=0, tiled=True
    ).reshape(peers * 4, LANES)
    own, edge, base, depth, speed, rate = call(
        base_kernel,
        (
            shape((cells, cells), BF16),
            shape((2 * HALO, cells), BF16),
            shape((levels, cells), F32),
            shape((levels, LANES), F32),
            shape((levels, LANES), F32),
            shape((levels, LANES), F32),
        ),
        [SMEM, VMEM, VMEM, VMEM],
        (VMEM,) * 6,
        flops=1_000_000_000,
    )(kappa, neighbours, tracer, mask)
    heat, forced, halo = call(
        heat_kernel,
        (shape((1, cells), F32), shape((levels, LANES), F32), shape((1, LANES), F32)),
        [VMEM] * 7,
        (VMEM,) * 3,
        [pltpu.VMEM((peers * 4, LANES), F32)],
    )(returned, chosen, here, before, after, mask, depth)
    swapped = lax.ppermute(forced, axes, seams + [(target, source) for source, target in seams])
    part, fluxes = call(
        partial_kernel,
        (shape((levels, cells), F32), shape((rows, atm_cells), BF16)),
        [VMEM] * 7,
        (VMEM, VMEM),
        flops=100_000_000,
    )(heat, own, base, mask, depth, rate, fluxes)
    tracer_out = call(finish_kernel, shape((levels, cells), F32), [VMEM] * 8, VMEM)(
        halo, swapped, before, after, edge, part, speed, rate
    )
    return (fluxes, tracer_out)


def solution(mesh):
    split = ("grp", "blk")
    return jax.shard_map(
        shards,
        mesh=mesh,
        in_specs=(
            P(None, split),
            P(split),
            P(split),
            P(split, None),
            P(split),
            P(split, None),
            P(None, split),
            P(split),
            P(),
            P(),
            P(),
            P(None, split),
            P(None, split),
        ),
        out_specs=(P(None, split), P(None, split)),
        check_vma=False,
    )
```

```python
import jax
import jax.numpy as jnp
from jax import lax
from jax.experimental import pallas as pl
from jax.experimental.pallas import tpu as pltpu
from jax.sharding import PartitionSpec as P

TILE = 64
HALO = 64
LANES = 128
PITCH = 33
F32 = jnp.float32
BF16 = jnp.bfloat16
SMEM = pl.BlockSpec(memory_space=pltpu.SMEM)
VMEM = pl.BlockSpec(memory_space=pltpu.VMEM)
HBM = pl.BlockSpec(memory_space=pltpu.HBM)


def iota(shape, dim):
    return lax.broadcasted_iota(jnp.int32, shape, dim)


def parts(value, count):
    out = []
    for _ in range(count - 1):
        high = value.astype(BF16).astype(F32)
        out.append(high)
        value = value - high
    out.append(value)
    return jnp.concatenate(out, axis=0).astype(BF16)


def column(scalars, count, rows):
    where = iota((rows, LANES), 0)
    out = jnp.zeros((rows, LANES), F32)
    for i in range(count):
        out = jnp.where(where == i, scalars[i], out)
    return out


def mm(a, b):
    return jnp.dot(a, b, preferred_element_type=F32)


def line(block):
    return jnp.concatenate([block[i : i + 1, :] for i in range(block.shape[0])], axis=1)


def across(col, width):
    return jnp.concatenate([col] * (width // LANES), axis=1)


def pack_kernel(
    src_hbm, route_hbm, tile_hbm, fields_hbm, mask_hbm, couple_hbm, weights_hbm, out,
    src, route, tile, fields, mask, couple, weights, tiles, wide, slots, seen, sems,
):
    pairs = (
        (fields_hbm, fields),
        (mask_hbm, mask),
        (couple_hbm, couple),
        (route_hbm, route),
        (src_hbm, src),
        (tile_hbm, tile),
        (weights_hbm, weights),
    )
    copies = [pltpu.make_async_copy(a, b, sems.at[i]) for i, (a, b) in enumerate(pairs)]
    for copy in copies:
        copy.start()
    entries = weights.shape[0]
    rows = couple.shape[0]
    half = rows // 2
    slots[...] = jnp.zeros(slots.shape, F32)
    for copy in copies[:3]:
        copy.wait()
    mixed = mm(parts(couple[...], 3), fields[...])
    mixed = mixed[:rows] + mixed[rows : 2 * rows] + mixed[2 * rows :]
    mixed = mixed * line(mask[...].astype(F32))
    high = mixed.astype(BF16).astype(F32)
    low = mixed - high
    flip = lambda x: jnp.concatenate([x[half:], x[:half]], axis=0)
    straight = jnp.concatenate([high, low], axis=0)
    swapped = jnp.concatenate([flip(high), flip(low)], axis=0)
    count = mixed.shape[1] // LANES
    stacks = [
        jnp.concatenate([x[:, j * LANES : (j + 1) * LANES] for j in range(count)], axis=0).astype(BF16)
        for x in (straight, swapped)
    ]
    for k in range(4):
        wanted = iota((LANES, TILE // 2), 1) * 2 + ((k // 2) * TILE + k % 2)
        pick = (iota((LANES, TILE // 2), 0) == wanted).astype(F32).astype(BF16)
        part = mm(stacks[k % 2], pick).astype(BF16)
        at = (k % 2) * 2 * rows
        for j in range(count):
            tiles[2 * j + k // 2, at : at + 2 * rows, :] = part[2 * rows * j : 2 * rows * (j + 1)]
    for copy in copies[3:]:
        copy.wait()
    for e in range(entries):
        seen[route[e]] = 0
    flat = weights[...].astype(F32)
    for g in range(entries // 8):
        for j in range(TILE // 2):
            wide[pl.ds(g * 8 * PITCH + j, 8, stride=PITCH), :] = flat[
                g * 8 : (g + 1) * 8, j * LANES : (j + 1) * LANES
            ]
    left = iota((rows, LANES), 1) < TILE
    for e in range(entries):
        to = route[e]
        rank = seen[to]
        seen[to] = rank + 1
        at = (to * 2 + rank) * (half + 1)
        sent = mm(tiles[src[e]], wide[e * PITCH : e * PITCH + TILE // 2, :].astype(BF16))
        even = sent[:rows] + sent[rows : 2 * rows]
        odd = sent[2 * rows : 3 * rows] + sent[3 * rows :]
        both = jnp.where(left, even, odd)
        slots[pl.ds(at, half), :] = both[:half] + pltpu.roll(both, TILE, 1)[half:]
        slots[pl.ds(at + half, 1), :] = jnp.full((1, LANES), tile[e] + 1, jnp.int32).astype(F32)
    out[...] = slots[...].astype(BF16)


def ship_kernel(src, route, flipped, tracer, mask, out, seen):
    entries = src.shape[0]
    levels, cells = tracer.shape
    half = entries * TILE // 2
    for e in range(entries):
        seen[route[e]] = 0
    slots = []
    for e in range(entries):
        to = route[e]
        rank = seen[to]
        seen[to] = rank + 1
        slots.append(to * 2 + rank)
    out[:half, :] = jnp.concatenate([flipped[:half, :], flipped[half:, :]], axis=1)
    ends = lambda x: jnp.concatenate([x[:, cells - HALO :], x[:, :HALO]], axis=1)
    sea = ends(line(mask[...].astype(F32)))
    edge = ends(tracer[...]) * sea
    out[half : half + 32, :] = jnp.concatenate(
        [edge, jnp.broadcast_to(sea, (32 - levels, LANES))], axis=0
    ).astype(BF16)
    where = iota((32, LANES), 0)
    slot_rows = jnp.full((32, LANES), -1, jnp.int32)
    tile_rows = jnp.full((32, LANES), -1, jnp.int32)
    for e in range(entries):
        here = where == (e // 2 + 16 * (e % 2))
        slot_rows = jnp.where(here, slots[e], slot_rows)
        tile_rows = jnp.where(here, src[e], tile_rows)
    out[half + 32 : half + 64, :] = slot_rows.astype(F32).astype(BF16)
    out[half + 64 : half + 96, :] = tile_rows.astype(F32).astype(BF16)


def tables_kernel(src, state, frac, couple, mixed, shares, chosen):
    entries = src.shape[0]
    rows = couple.shape[0]
    half = rows // 2
    part = mm(parts(couple[...], 3), state[...])
    part = part[:rows] + part[rows : 2 * rows] + part[2 * rows :]
    mixed[...] = jnp.zeros(mixed.shape, F32)
    shares[...] = jnp.zeros(shares.shape, F32)
    low = iota((half, LANES), 1) < TILE
    for i in range(state.shape[1] // LANES):
        here = part[:, i * LANES : (i + 1) * LANES]
        there = pltpu.roll(here, TILE, 1)
        one = jnp.where(low, here[:half], there[half:])
        two = jnp.where(low, there[:half], here[half:])
        for q in range(half):
            at = slice(q * LANES, (q + 1) * LANES)
            mixed[2 * i : 2 * i + 1, at] = one[q : q + 1]
            mixed[2 * i + 1 : 2 * i + 2, at] = two[q : q + 1]
        here = frac[i : i + 1, :]
        there = pltpu.roll(here, TILE, 1)
        shares[2 * i : 2 * i + 1, :] = jnp.where(low[:1], here, there)
        shares[2 * i + 1 : 2 * i + 2, :] = jnp.where(low[:1], there, here)

    low = iota((16, LANES), 1) < TILE
    for j in range(entries // 2):
        owner = jnp.where(low, src[2 * j], src[2 * j + 1])
        chosen[:, j * LANES : (j + 1) * LANES] = (iota((16, LANES), 0) == owner).astype(F32)


def merge_kernel(heat_coef, got, mixed, shares, fluxes, back, flat):
    half = mixed.shape[1] // LANES
    peers = back.shape[0] // 4
    pitch = 2 * (half + 1)
    flat[...] = got[...].astype(F32)
    row = lambda rank, q: flat[pl.ds(rank * (half + 1) + q, peers, stride=pitch), :]
    first, second = row(0, half), row(1, half)
    named = jnp.concatenate([first, second], axis=0).astype(BF16)
    pick = (iota((16, LANES), 1) == 0).astype(F32).astype(BF16)
    ids = lax.dot_general(pick, named, (((1,), (1,)), ((), ())), preferred_element_type=F32)
    member = (ids == (iota(ids.shape, 0) + 1).astype(F32)).astype(F32).astype(BF16)
    values = jnp.concatenate(
        [jnp.concatenate([row(0, q), row(1, q)], axis=0) for q in range(half)], axis=1
    ).astype(BF16)
    remap = mm(member, values)
    low = iota((1, LANES), 1) < TILE
    heat = jnp.zeros((16, LANES), F32)
    for q in range(half):
        at = slice(q * LANES, (q + 1) * LANES)
        flux = ((mixed[:, at] - remap[:, at]) * shares[...]).astype(BF16).astype(F32)
        fluxes[:, at] = flux
        heat = heat + flux * jnp.where(low, heat_coef[q], heat_coef[q + half])
    heat = heat + pltpu.roll(heat, TILE, 1)
    high = heat.astype(BF16).astype(F32)
    heat = jnp.concatenate([high, heat - high], axis=0)
    blank = jnp.zeros((32, LANES), F32)
    spread = jnp.concatenate(
        [jnp.where(low, heat, 0.0), blank, jnp.where(low, 0.0, heat), blank], axis=0
    ).astype(BF16)
    lane = iota((peers, LANES), 1)
    target = jnp.where((lane & (TILE - 1)) < 32, (lane & 15) + 1, -1).astype(F32)
    asked = jnp.where(lane < TILE, first, second)
    reply = mm((asked == target).astype(F32).astype(BF16), spread)
    high = reply.astype(BF16).astype(F32)
    four = (high, reply - high, pltpu.roll(high, 1, 0), pltpu.roll(high, peers - 1, 0))
    for k, rows in enumerate(four):
        flat[pl.ds(k, peers, stride=4), :] = rows
    back[...] = flat[: 4 * peers, :].astype(BF16)


def base_kernel(kappa, near, tracer, mask, own, edge, base, depth, speed, rate):
    levels, cells = tracer.shape
    place = iota((LANES, cells), 0).astype(F32).astype(BF16)

    def counts(start):
        total = jnp.zeros(place.shape, BF16)
        for k in range(near.shape[0]):
            at = jnp.clip(near[k : k + 1, :] - start, -1, LANES).astype(F32).astype(BF16)
            total = total + jnp.where(at == place, jnp.ones((), BF16), jnp.zeros((), BF16))
        return total

    @pl.loop(0, cells // LANES)
    def _(i):
        at = pl.multiple_of(i * LANES, LANES)
        own[pl.ds(at, LANES), :] = counts(at + HALO)

    sea = line(mask[...].astype(F32))
    land = sea.astype(BF16)
    edge[:HALO, :] = (land * counts(0))[:HALO]
    edge[HALO:, :] = (land * counts(cells + HALO))[:HALO]

    value = tracer[...]
    pad = jnp.zeros((32 - levels, cells), F32)
    total = mm(parts(jnp.concatenate([value * sea, pad], axis=0), 2), own[...])
    total = sea * ((total[:32] + total[32:])[:levels] - 6.0 * value)
    pace = column(kappa, levels, levels)
    deep = jnp.exp(-iota((levels, LANES), 0).astype(F32) / 10.0)
    depth[...] = deep
    speed[...] = pace
    rate[...] = deep * pace
    base[...] = value + across(pace, cells) * total


def in_group(shape):
    me = lax.axis_index("blk")
    low = iota(shape, 1) < TILE
    return jnp.where(low, me, lax.axis_size("blk") - 1 - me) > 0


def heat_kernel(got, chosen, here, before, after, mask, depth, heat, forced, halo, flat):
    cells = heat.shape[1]
    half = here.shape[0] - 96
    lane = iota((32, LANES), 1)
    target = ((lane & (TILE - 1)) * 2 + (lane >> 6)).astype(F32)
    meta = lambda ref, at: ref[half + at : half + at + 32, :].astype(F32)
    found = lambda ref: meta(ref, 32) == target
    last = float(cells // TILE - 1)
    picks = [
        pick.astype(F32).astype(BF16)
        for pick in (
            found(here),
            found(before) & (meta(before, 64) == last),
            found(after) & (meta(after, 64) == 0.0),
        )
    ]
    peers = got.shape[0] // 4
    count = half // LANES
    flat[...] = got[...].astype(F32)
    low = iota((16, LANES), 1) < TILE

    def lookup(k, which):
        rows = flat[pl.ds(k, peers, stride=4), :]
        turned = pltpu.roll(rows, TILE, 1)
        one = jnp.concatenate([rows, turned], axis=0).astype(BF16)
        two = jnp.concatenate([turned, rows], axis=0).astype(BF16)
        return jnp.where(low, mm(picks[which][:16], one), mm(picks[which][16:], two))

    def laid(rows, start):
        return jnp.concatenate([rows[j : j + 1] for j in range(start, start + count)], axis=1)

    high, rest = lookup(0, 0), lookup(1, 0)
    previous, following = lookup(2, 1), lookup(3, 2)
    spread = []
    for h in range(2):
        pick = chosen[:, h * half : (h + 1) * half]
        for rows in (high, rest):
            spread.append(pick * laid(rows, h * count))
    summed = mm(jnp.concatenate(spread, axis=0).astype(BF16), here[:half, :])
    summed = summed[:16] + summed[16:32] + pltpu.roll(summed[32:48] + summed[48:], TILE, 1)
    blank = jnp.zeros((14, half), F32)

    def side(rows, ref):
        rows = jnp.concatenate([laid(rows, 0), laid(rows, count), blank], axis=0)
        return mm(rows.astype(BF16), ref[:half, :])

    left, right = side(previous, before), side(following, after)
    left = left[0:1] + pltpu.roll(left, TILE, 1)[1:2]
    right = right[1:2] + pltpu.roll(right, TILE, 1)[0:1]
    levels = depth.shape[0]
    coast = jnp.where(low[:1], meta(before, 0)[levels : levels + 1], meta(after, 0)[levels : levels + 1])
    beside = jnp.where(low[:1], left, right) * coast
    halo[...] = beside
    edges = jnp.where(lane < TILE, meta(before, 0), meta(after, 0))[:levels]
    deep = depth[...]
    beside = edges + deep * beside
    row = jnp.concatenate([summed[t : t + 1, :TILE] for t in range(cells // TILE)], axis=1)
    row = row * line(mask[...].astype(F32))
    heat[...] = row
    ends = jnp.concatenate([row[:, cells - HALO :], row[:, :HALO]], axis=1)
    ends = meta(here, 0)[:levels] + deep * ends
    forced[...] = jnp.where(lax.axis_index("grp") == 0, ends, beside)


def halves(row):
    high = row.astype(BF16).astype(F32)
    blank = jnp.zeros((14, row.shape[1]), F32)
    return jnp.concatenate([high, row - high, blank], axis=0).astype(BF16)


def partial_kernel(heat, own, base, mask, depth, rate, fluxes, out, placed):
    half = placed.shape[0] // 2
    low = iota((half, LANES), 1) < TILE
    for i in range(placed.shape[1] // LANES):
        piece = lambda t: jnp.concatenate(
            [fluxes[t : t + 1, q * LANES : (q + 1) * LANES] for q in range(half)], axis=0
        )
        one, two = piece(2 * i), piece(2 * i + 1)
        block = jnp.concatenate(
            [
                jnp.where(low, one, pltpu.roll(two, TILE, 1)),
                jnp.where(low, pltpu.roll(one, TILE, 1), two),
            ],
            axis=0,
        )
        placed[:, i * LANES : (i + 1) * LANES] = block.astype(BF16)
    cells = base.shape[1]
    sea = line(mask[...].astype(F32))
    row = heat[...]
    near = mm(halves(row), own[...])
    near = sea * (near[0:1] + near[1:2] - 6.0 * row)
    out[...] = base[...] + across(depth[...], cells) * row + across(rate[...], cells) * near


def finish_kernel(halo, swapped, before, after, edge, part, speed, rate, out):
    levels, cells = part.shape
    first = before.shape[0] - 96
    rows = slice(first, first + 32)
    low = iota((32, LANES), 1) < TILE
    outer = jnp.where(low, before[rows, :].astype(F32), after[rows, :].astype(F32))[:levels]
    outer = jnp.where(in_group((levels, LANES)), outer, swapped[...]) * speed[...]
    pad = jnp.zeros((32 - levels, LANES), F32)
    outer = parts(jnp.concatenate([outer, pad], axis=0), 2)
    inner = halves(jnp.where(in_group((1, LANES)), halo[...], 0.0))
    near = mm(jnp.concatenate([outer, inner], axis=0), edge[...])
    inner = near[64:65] + near[65:66]
    out[...] = part[...] + (near[:32] + near[32:64])[:levels] + across(rate[...], cells) * inner


def call(kernel, out_shape, in_specs, out_specs, scratch=(), flops=1_000_000, vmem=24 * 2**20):
    return pl.pallas_call(
        kernel,
        out_shape=out_shape,
        in_specs=in_specs,
        out_specs=out_specs,
        scratch_shapes=list(scratch),
        cost_estimate=pl.CostEstimate(flops=flops, bytes_accessed=2_000_000, transcendentals=0),
        compiler_params=pltpu.CompilerParams(vmem_limit_bytes=vmem),
    )


def shards(
    ocean_fields,
    ocean_mask,
    entry_src,
    entry_route,
    entry_tile,
    weight_tiles,
    atm_state,
    atm_frac,
    couple,
    heat_coef,
    kappa,
    tracer,
    neighbours,
):
    fields, cells = ocean_fields.shape
    entries = entry_src.shape[0]
    atm_cells = atm_state.shape[1]
    rows = couple.shape[0]
    levels = tracer.shape[0]
    peers = lax.axis_size("blk")
    shape = jax.ShapeDtypeStruct
    half = rows // 2
    mask = ocean_mask.reshape(cells // LANES, LANES)
    route = entry_route.reshape(entries)
    pitch = 2 * (half + 1)
    i32 = jnp.int32
    sent = call(
        pack_kernel,
        shape((peers * pitch, LANES), BF16),
        [HBM] * 7,
        VMEM,
        [
            pltpu.SMEM((entries,), i32),
            pltpu.SMEM((entries,), i32),
            pltpu.SMEM((entries,), i32),
            pltpu.VMEM((fields, cells), BF16),
            pltpu.VMEM((cells // LANES, LANES), i32),
            pltpu.VMEM((rows, fields), F32),
            pltpu.VMEM((entries, TILE * TILE), BF16),
            pltpu.VMEM((cells // TILE, 4 * rows, TILE // 2), BF16),
            pltpu.VMEM((entries * PITCH, LANES), F32),
            pltpu.VMEM((peers * pitch, LANES), F32),
            pltpu.SMEM((peers,), i32),
            pltpu.SemaphoreType.DMA((7,)),
        ],
        vmem=64 * 2**20,
    )(entry_src, route, entry_tile, ocean_fields, mask, couple, weight_tiles)
    sent, weight_tiles, neighbours, atm_state, tracer = lax.optimization_barrier(
        (sent, weight_tiles, neighbours, atm_state, tracer)
    )
    got = lax.all_to_all(
        sent.reshape(peers, half + 1, 2, LANES), "blk", split_axis=0, concat_axis=0, tiled=True
    ).reshape(peers * pitch, LANES)
    flipped = weight_tiles.reshape(entries, TILE, TILE).transpose(0, 2, 1)
    here = call(
        ship_kernel,
        shape((entries * TILE // 2 + 96, LANES), BF16),
        [SMEM, SMEM, VMEM, VMEM, VMEM],
        VMEM,
        [pltpu.SMEM((peers,), i32)],
    )(entry_src, route, flipped.reshape(entries * TILE, TILE), tracer, mask)
    axes = ("grp", "blk")
    count = lax.axis_size(axes)
    up = [(i, i - i % peers + (i + 1) % peers) for i in range(count)]
    down = [(target, source) for source, target in up]
    seams = [(i, (i + peers) % count) for i in range(peers, count, peers)] + [(0, count - 1)]
    seams += [(i, i - peers) for i in range(2 * peers - 1, count, peers)] + [(peers - 1, peers)]
    before = lax.ppermute(here, axes, up)
    after = lax.ppermute(here, axes, down)
    mixed, shares, chosen = call(
        tables_kernel,
        (
            shape((16, half * LANES), F32),
            shape((16, LANES), F32),
            shape((16, entries * TILE), F32),
        ),
        [SMEM, VMEM, VMEM, VMEM],
        (VMEM,) * 3,
    )(entry_src, atm_state, atm_frac.reshape(atm_cells // LANES, LANES), couple)
    fluxes, back = call(
        merge_kernel,
        (shape((16, half * LANES), F32), shape((peers * 4, LANES), BF16)),
        [SMEM, VMEM, VMEM, VMEM],
        (VMEM, VMEM),
        [pltpu.VMEM((peers * pitch, LANES), F32)],
    )(heat_coef, got, mixed, shares)
    back, neighbours, tracer = lax.optimization_barrier((back, neighbours, tracer))
    returned = lax.all_to_all(
        back.reshape(peers, 2, 2, LANES), "blk", split_axis=0, concat_axis=0, tiled=True
    ).reshape(peers * 4, LANES)
    own, edge, base, depth, speed, rate = call(
        base_kernel,
        (
            shape((cells, cells), BF16),
            shape((2 * HALO, cells), BF16),
            shape((levels, cells), F32),
            shape((levels, LANES), F32),
            shape((levels, LANES), F32),
            shape((levels, LANES), F32),
        ),
        [SMEM, VMEM, VMEM, VMEM],
        (VMEM,) * 6,
        flops=1_000_000_000,
    )(kappa, neighbours, tracer, mask)
    heat, forced, halo = call(
        heat_kernel,
        (shape((1, cells), F32), shape((levels, LANES), F32), shape((1, LANES), F32)),
        [VMEM] * 7,
        (VMEM,) * 3,
        [pltpu.VMEM((peers * 4, LANES), F32)],
    )(returned, chosen, here, before, after, mask, depth)
    swapped = lax.ppermute(forced, axes, seams)
    part, fluxes = call(
        partial_kernel,
        (shape((levels, cells), F32), shape((rows, atm_cells), BF16)),
        [VMEM] * 7,
        (VMEM, VMEM),
        flops=100_000_000,
    )(heat, own, base, mask, depth, rate, fluxes)
    tracer_out = call(finish_kernel, shape((levels, cells), F32), [VMEM] * 8, VMEM)(
        halo, swapped, before, after, edge, part, speed, rate
    )
    return (fluxes, tracer_out)


def solution(mesh):
    split = ("grp", "blk")
    return jax.shard_map(
        shards,
        mesh=mesh,
        in_specs=(
            P(None, split),
            P(split),
            P(split),
            P(split, None),
            P(split),
            P(split, None),
            P(None, split),
            P(split),
            P(),
            P(),
            P(),
            P(None, split),
            P(None, split),
        ),
        out_specs=(P(None, split), P(None, split)),
        check_vma=False,
    )
```

```python
import jax
import jax.numpy as jnp
from jax import lax
from jax.experimental import pallas as pl
from jax.experimental.pallas import tpu as pltpu
from jax.sharding import PartitionSpec as P

TILE = 64
HALO = 64
LANES = 128
PITCH = 33
WIDE = 65
F32 = jnp.float32
BF16 = jnp.bfloat16
SMEM = pl.BlockSpec(memory_space=pltpu.SMEM)
VMEM = pl.BlockSpec(memory_space=pltpu.VMEM)
HBM = pl.BlockSpec(memory_space=pltpu.HBM)


def iota(shape, dim):
    return lax.broadcasted_iota(jnp.int32, shape, dim)


def parts(value, count):
    out = []
    for _ in range(count - 1):
        high = value.astype(BF16).astype(F32)
        out.append(high)
        value = value - high
    out.append(value)
    return jnp.concatenate(out, axis=0).astype(BF16)


def column(scalars, count, rows):
    where = iota((rows, LANES), 0)
    out = jnp.zeros((rows, LANES), F32)
    for i in range(count):
        out = jnp.where(where == i, scalars[i], out)
    return out


def mm(a, b):
    return jnp.dot(a, b, preferred_element_type=F32)


def line(block):
    return jnp.concatenate([block[i : i + 1, :] for i in range(block.shape[0])], axis=1)


def across(col, width):
    return jnp.concatenate([col] * (width // LANES), axis=1)


def pack_kernel(
    src_hbm, route_hbm, tile_hbm, fields_hbm, mask_hbm, couple_hbm, weights_hbm, out,
    src, route, tile, fields, mask, couple, weights, tiles, wide, slots, seen, sems,
):
    pairs = (
        (fields_hbm, fields),
        (mask_hbm, mask),
        (couple_hbm, couple),
        (route_hbm, route),
        (src_hbm, src),
        (tile_hbm, tile),
        (weights_hbm, weights),
    )
    copies = [pltpu.make_async_copy(a, b, sems.at[i]) for i, (a, b) in enumerate(pairs)]
    for copy in copies:
        copy.start()
    entries = weights.shape[0]
    rows = couple.shape[0]
    half = rows // 2
    slots[...] = jnp.zeros(slots.shape, F32)
    for copy in copies[:3]:
        copy.wait()
    mixed = mm(parts(couple[...], 3), fields[...])
    mixed = mixed[:rows] + mixed[rows : 2 * rows] + mixed[2 * rows :]
    mixed = mixed * line(mask[...].astype(F32))
    high = mixed.astype(BF16).astype(F32)
    low = mixed - high
    flip = lambda x: jnp.concatenate([x[half:], x[:half]], axis=0)
    straight = jnp.concatenate([high, low], axis=0)
    swapped = jnp.concatenate([flip(high), flip(low)], axis=0)
    count = mixed.shape[1] // LANES
    stacks = [
        jnp.concatenate([x[:, j * LANES : (j + 1) * LANES] for j in range(count)], axis=0).astype(BF16)
        for x in (straight, swapped)
    ]
    for k in range(4):
        wanted = iota((LANES, TILE // 2), 1) * 2 + ((k // 2) * TILE + k % 2)
        pick = (iota((LANES, TILE // 2), 0) == wanted).astype(F32).astype(BF16)
        part = mm(stacks[k % 2], pick).astype(BF16)
        at = (k % 2) * 2 * rows
        for j in range(count):
            tiles[2 * j + k // 2, at : at + 2 * rows, :] = part[2 * rows * j : 2 * rows * (j + 1)]
    for copy in copies[3:]:
        copy.wait()
    for e in range(entries):
        seen[route[e]] = 0
    flat = weights[...].astype(F32)
    for g in range(entries // 8):
        for j in range(TILE // 2):
            wide[pl.ds(g * 8 * PITCH + j, 8, stride=PITCH), :] = flat[
                g * 8 : (g + 1) * 8, j * LANES : (j + 1) * LANES
            ]
    left = iota((rows, LANES), 1) < TILE
    for e in range(entries):
        to = route[e]
        rank = seen[to]
        seen[to] = rank + 1
        at = (to * 2 + rank) * (half + 1)
        sent = mm(tiles[src[e]], wide[e * PITCH : e * PITCH + TILE // 2, :].astype(BF16))
        even = sent[:rows] + sent[rows : 2 * rows]
        odd = sent[2 * rows : 3 * rows] + sent[3 * rows :]
        both = jnp.where(left, even, odd)
        slots[pl.ds(at, half), :] = both[:half] + pltpu.roll(both, TILE, 1)[half:]
        slots[pl.ds(at + half, 1), :] = jnp.full((1, LANES), tile[e] + 1, jnp.int32).astype(F32)
    out[...] = slots[...].astype(BF16)


def ship_kernel(src, route, weights, tracer, mask, out, seen, wide):
    entries = src.shape[0]
    levels, cells = tracer.shape
    half = entries * TILE // 2
    for e in range(entries):
        seen[route[e]] = 0
    slots = []
    for e in range(entries):
        to = route[e]
        rank = seen[to]
        seen[to] = rank + 1
        slots.append(to * 2 + rank)
    flat = weights[...].astype(F32)
    low = iota((8, LANES), 1) < TILE
    for g in range(entries // 8):
        for j in range(TILE // 2):
            block = flat[g * 8 : (g + 1) * 8, j * LANES : (j + 1) * LANES]
            at = g * 8 * WIDE + 2 * j
            wide[pl.ds(at, 8, stride=WIDE), :] = jnp.where(low, block, 0.0)
            wide[pl.ds(at + 1, 8, stride=WIDE), :] = jnp.where(low, 0.0, block)
    eye = iota((TILE, LANES), 0) == (iota((TILE, LANES), 1) & (TILE - 1))
    eye = eye.astype(F32).astype(BF16)
    for e in range(entries // 2):
        pair = [wide[i * WIDE : i * WIDE + TILE, :] for i in (e, e + entries // 2)]
        rows = jnp.concatenate(pair, axis=0).astype(BF16)
        turned = lax.dot_general(eye, rows, (((1,), (1,)), ((), ())), preferred_element_type=F32)
        out[e * TILE : (e + 1) * TILE, :] = turned.astype(BF16)
    ends = lambda x: jnp.concatenate([x[:, cells - HALO :], x[:, :HALO]], axis=1)
    sea = ends(line(mask[...].astype(F32)))
    edge = ends(tracer[...]) * sea
    out[half : half + 32, :] = jnp.concatenate(
        [edge, jnp.broadcast_to(sea, (32 - levels, LANES))], axis=0
    ).astype(BF16)
    where = iota((32, LANES), 0)
    slot_rows = jnp.full((32, LANES), -1, jnp.int32)
    tile_rows = jnp.full((32, LANES), -1, jnp.int32)
    for e in range(entries):
        here = where == (e // 2 + 16 * (e % 2))
        slot_rows = jnp.where(here, slots[e], slot_rows)
        tile_rows = jnp.where(here, src[e], tile_rows)
    out[half + 32 : half + 64, :] = slot_rows.astype(F32).astype(BF16)
    out[half + 64 : half + 96, :] = tile_rows.astype(F32).astype(BF16)


def tables_kernel(src, state, frac, couple, mixed, shares, chosen):
    entries = src.shape[0]
    rows = couple.shape[0]
    half = rows // 2
    part = mm(parts(couple[...], 3), state[...])
    part = part[:rows] + part[rows : 2 * rows] + part[2 * rows :]
    mixed[...] = jnp.zeros(mixed.shape, F32)
    shares[...] = jnp.zeros(shares.shape, F32)
    low = iota((half, LANES), 1) < TILE
    for i in range(state.shape[1] // LANES):
        here = part[:, i * LANES : (i + 1) * LANES]
        there = pltpu.roll(here, TILE, 1)
        one = jnp.where(low, here[:half], there[half:])
        two = jnp.where(low, there[:half], here[half:])
        for q in range(half):
            at = slice(q * LANES, (q + 1) * LANES)
            mixed[2 * i : 2 * i + 1, at] = one[q : q + 1]
            mixed[2 * i + 1 : 2 * i + 2, at] = two[q : q + 1]
        here = frac[i : i + 1, :]
        there = pltpu.roll(here, TILE, 1)
        shares[2 * i : 2 * i + 1, :] = jnp.where(low[:1], here, there)
        shares[2 * i + 1 : 2 * i + 2, :] = jnp.where(low[:1], there, here)

    low = iota((16, LANES), 1) < TILE
    for j in range(entries // 2):
        owner = jnp.where(low, src[2 * j], src[2 * j + 1])
        chosen[:, j * LANES : (j + 1) * LANES] = (iota((16, LANES), 0) == owner).astype(F32)


def merge_kernel(heat_coef, got, mixed, shares, fluxes, back, flat):
    half = mixed.shape[1] // LANES
    peers = back.shape[0] // 4
    pitch = 2 * (half + 1)
    flat[...] = got[...].astype(F32)
    row = lambda rank, q: flat[pl.ds(rank * (half + 1) + q, peers, stride=pitch), :]
    first, second = row(0, half), row(1, half)
    named = jnp.concatenate([first, second], axis=0).astype(BF16)
    pick = (iota((16, LANES), 1) == 0).astype(F32).astype(BF16)
    ids = lax.dot_general(pick, named, (((1,), (1,)), ((), ())), preferred_element_type=F32)
    member = (ids == (iota(ids.shape, 0) + 1).astype(F32)).astype(F32).astype(BF16)
    values = jnp.concatenate(
        [jnp.concatenate([row(0, q), row(1, q)], axis=0) for q in range(half)], axis=1
    ).astype(BF16)
    remap = mm(member, values)
    low = iota((1, LANES), 1) < TILE
    heat = jnp.zeros((16, LANES), F32)
    for q in range(half):
        at = slice(q * LANES, (q + 1) * LANES)
        flux = ((mixed[:, at] - remap[:, at]) * shares[...]).astype(BF16).astype(F32)
        fluxes[:, at] = flux
        heat = heat + flux * jnp.where(low, heat_coef[q], heat_coef[q + half])
    heat = heat + pltpu.roll(heat, TILE, 1)
    high = heat.astype(BF16).astype(F32)
    heat = jnp.concatenate([high, heat - high], axis=0)
    blank = jnp.zeros((32, LANES), F32)
    spread = jnp.concatenate(
        [jnp.where(low, heat, 0.0), blank, jnp.where(low, 0.0, heat), blank], axis=0
    ).astype(BF16)
    lane = iota((peers, LANES), 1)
    target = jnp.where((lane & (TILE - 1)) < 32, (lane & 15) + 1, -1).astype(F32)
    asked = jnp.where(lane < TILE, first, second)
    reply = mm((asked == target).astype(F32).astype(BF16), spread)
    high = reply.astype(BF16).astype(F32)
    four = (high, reply - high, pltpu.roll(high, 1, 0), pltpu.roll(high, peers - 1, 0))
    for k, rows in enumerate(four):
        flat[pl.ds(k, peers, stride=4), :] = rows
    back[...] = flat[: 4 * peers, :].astype(BF16)


def base_kernel(kappa, near, tracer, mask, own, edge, base, depth, speed, rate):
    levels, cells = tracer.shape
    place = iota((LANES, cells), 0).astype(F32).astype(BF16)

    def counts(start):
        total = jnp.zeros(place.shape, BF16)
        for k in range(near.shape[0]):
            at = jnp.clip(near[k : k + 1, :] - start, -1, LANES).astype(F32).astype(BF16)
            total = total + jnp.where(at == place, jnp.ones((), BF16), jnp.zeros((), BF16))
        return total

    @pl.loop(0, cells // LANES)
    def _(i):
        at = pl.multiple_of(i * LANES, LANES)
        own[pl.ds(at, LANES), :] = counts(at + HALO)

    sea = line(mask[...].astype(F32))
    land = sea.astype(BF16)
    edge[:HALO, :] = (land * counts(0))[:HALO]
    edge[HALO:, :] = (land * counts(cells + HALO))[:HALO]

    value = tracer[...]
    pad = jnp.zeros((32 - levels, cells), F32)
    total = mm(parts(jnp.concatenate([value * sea, pad], axis=0), 2), own[...])
    total = sea * ((total[:32] + total[32:])[:levels] - 6.0 * value)
    pace = column(kappa, levels, levels)
    deep = jnp.exp(-iota((levels, LANES), 0).astype(F32) / 10.0)
    depth[...] = deep
    speed[...] = pace
    rate[...] = deep * pace
    base[...] = value + across(pace, cells) * total


def in_group(shape):
    me = lax.axis_index("blk")
    low = iota(shape, 1) < TILE
    return jnp.where(low, me, lax.axis_size("blk") - 1 - me) > 0


def heat_kernel(got, chosen, here, before, after, mask, depth, heat, forced, halo, flat):
    cells = heat.shape[1]
    half = here.shape[0] - 96
    lane = iota((32, LANES), 1)
    target = ((lane & (TILE - 1)) * 2 + (lane >> 6)).astype(F32)
    meta = lambda ref, at: ref[half + at : half + at + 32, :].astype(F32)
    found = lambda ref: meta(ref, 32) == target
    last = float(cells // TILE - 1)
    picks = [
        pick.astype(F32).astype(BF16)
        for pick in (
            found(here),
            found(before) & (meta(before, 64) == last),
            found(after) & (meta(after, 64) == 0.0),
        )
    ]
    peers = got.shape[0] // 4
    count = half // LANES
    flat[...] = got[...].astype(F32)
    low = iota((16, LANES), 1) < TILE

    def lookup(k, which):
        rows = flat[pl.ds(k, peers, stride=4), :]
        turned = pltpu.roll(rows, TILE, 1)
        one = jnp.concatenate([rows, turned], axis=0).astype(BF16)
        two = jnp.concatenate([turned, rows], axis=0).astype(BF16)
        return jnp.where(low, mm(picks[which][:16], one), mm(picks[which][16:], two))

    def laid(rows, start):
        return jnp.concatenate([rows[j : j + 1] for j in range(start, start + count)], axis=1)

    high, rest = lookup(0, 0), lookup(1, 0)
    previous, following = lookup(2, 1), lookup(3, 2)
    spread = []
    for h in range(2):
        pick = chosen[:, h * half : (h + 1) * half]
        for rows in (high, rest):
            spread.append(pick * laid(rows, h * count))
    summed = mm(jnp.concatenate(spread, axis=0).astype(BF16), here[:half, :])
    summed = summed[:16] + summed[16:32] + pltpu.roll(summed[32:48] + summed[48:], TILE, 1)
    blank = jnp.zeros((14, half), F32)

    def side(rows, ref):
        rows = jnp.concatenate([laid(rows, 0), laid(rows, count), blank], axis=0)
        return mm(rows.astype(BF16), ref[:half, :])

    left, right = side(previous, before), side(following, after)
    left = left[0:1] + pltpu.roll(left, TILE, 1)[1:2]
    right = right[1:2] + pltpu.roll(right, TILE, 1)[0:1]
    levels = depth.shape[0]
    coast = jnp.where(low[:1], meta(before, 0)[levels : levels + 1], meta(after, 0)[levels : levels + 1])
    beside = jnp.where(low[:1], left, right) * coast
    halo[...] = beside
    edges = jnp.where(lane < TILE, meta(before, 0), meta(after, 0))[:levels]
    deep = depth[...]
    beside = edges + deep * beside
    row = jnp.concatenate([summed[t : t + 1, :TILE] for t in range(cells // TILE)], axis=1)
    row = row * line(mask[...].astype(F32))
    heat[...] = row
    ends = jnp.concatenate([row[:, cells - HALO :], row[:, :HALO]], axis=1)
    ends = meta(here, 0)[:levels] + deep * ends
    forced[...] = jnp.where(lax.axis_index("grp") == 0, ends, beside)


def halves(row):
    high = row.astype(BF16).astype(F32)
    blank = jnp.zeros((14, row.shape[1]), F32)
    return jnp.concatenate([high, row - high, blank], axis=0).astype(BF16)


def partial_kernel(heat, own, base, mask, depth, rate, fluxes, out, placed):
    half = placed.shape[0] // 2
    low = iota((half, LANES), 1) < TILE
    for i in range(placed.shape[1] // LANES):
        piece = lambda t: jnp.concatenate(
            [fluxes[t : t + 1, q * LANES : (q + 1) * LANES] for q in range(half)], axis=0
        )
        one, two = piece(2 * i), piece(2 * i + 1)
        block = jnp.concatenate(
            [
                jnp.where(low, one, pltpu.roll(two, TILE, 1)),
                jnp.where(low, pltpu.roll(one, TILE, 1), two),
            ],
            axis=0,
        )
        placed[:, i * LANES : (i + 1) * LANES] = block.astype(BF16)
    cells = base.shape[1]
    sea = line(mask[...].astype(F32))
    row = heat[...]
    near = mm(halves(row), own[...])
    near = sea * (near[0:1] + near[1:2] - 6.0 * row)
    out[...] = base[...] + across(depth[...], cells) * row + across(rate[...], cells) * near


def finish_kernel(halo, swapped, before, after, edge, part, speed, rate, out):
    levels, cells = part.shape
    first = before.shape[0] - 96
    rows = slice(first, first + 32)
    low = iota((32, LANES), 1) < TILE
    outer = jnp.where(low, before[rows, :].astype(F32), after[rows, :].astype(F32))[:levels]
    outer = jnp.where(in_group((levels, LANES)), outer, swapped[...]) * speed[...]
    pad = jnp.zeros((32 - levels, LANES), F32)
    outer = parts(jnp.concatenate([outer, pad], axis=0), 2)
    inner = halves(jnp.where(in_group((1, LANES)), halo[...], 0.0))
    near = mm(jnp.concatenate([outer, inner], axis=0), edge[...])
    inner = near[64:65] + near[65:66]
    out[...] = part[...] + (near[:32] + near[32:64])[:levels] + across(rate[...], cells) * inner


def call(kernel, out_shape, in_specs, out_specs, scratch=(), flops=2_000_000_000, vmem=24 * 2**20):
    return pl.pallas_call(
        kernel,
        out_shape=out_shape,
        in_specs=in_specs,
        out_specs=out_specs,
        scratch_shapes=list(scratch),
        cost_estimate=pl.CostEstimate(flops=flops, bytes_accessed=30_000_000, transcendentals=0),
        compiler_params=pltpu.CompilerParams(vmem_limit_bytes=vmem),
    )


def in_hbm(array):
    return pltpu.with_memory_space_constraint(array, pltpu.HBM)


def shards(
    ocean_fields,
    ocean_mask,
    entry_src,
    entry_route,
    entry_tile,
    weight_tiles,
    atm_state,
    atm_frac,
    couple,
    heat_coef,
    kappa,
    tracer,
    neighbours,
):
    fields, cells = ocean_fields.shape
    entries = entry_src.shape[0]
    atm_cells = atm_state.shape[1]
    rows = couple.shape[0]
    levels = tracer.shape[0]
    peers = lax.axis_size("blk")
    shape = jax.ShapeDtypeStruct
    half = rows // 2
    mask = ocean_mask.reshape(cells // LANES, LANES)
    route = entry_route.reshape(entries)
    pitch = 2 * (half + 1)
    i32 = jnp.int32
    sent = call(
        pack_kernel,
        shape((peers * pitch, LANES), BF16),
        [HBM] * 7,
        VMEM,
        [
            pltpu.SMEM((entries,), i32),
            pltpu.SMEM((entries,), i32),
            pltpu.SMEM((entries,), i32),
            pltpu.VMEM((fields, cells), BF16),
            pltpu.VMEM((cells // LANES, LANES), i32),
            pltpu.VMEM((rows, fields), F32),
            pltpu.VMEM((entries, TILE * TILE), BF16),
            pltpu.VMEM((cells // TILE, 4 * rows, TILE // 2), BF16),
            pltpu.VMEM((entries * PITCH, LANES), F32),
            pltpu.VMEM((peers * pitch, LANES), F32),
            pltpu.SMEM((peers,), i32),
            pltpu.SemaphoreType.DMA((7,)),
        ],
        vmem=64 * 2**20,
    )(entry_src, route, entry_tile, ocean_fields, mask, couple, weight_tiles)
    sent, weight_tiles, neighbours, atm_state, tracer = lax.optimization_barrier(
        (sent, weight_tiles, neighbours, atm_state, tracer)
    )
    got = lax.all_to_all(
        sent.reshape(peers, half + 1, 2, LANES), "blk", split_axis=0, concat_axis=0, tiled=True
    ).reshape(peers * pitch, LANES)
    here = call(
        ship_kernel,
        shape((entries * TILE // 2 + 96, LANES), BF16),
        [SMEM, SMEM, VMEM, VMEM, VMEM],
        VMEM,
        [pltpu.SMEM((peers,), i32), pltpu.VMEM((entries * WIDE, LANES), F32)],
    )(*(in_hbm(x) for x in (entry_src, route, weight_tiles, tracer, mask)))
    axes = ("grp", "blk")
    count = lax.axis_size(axes)
    up = [(i, i - i % peers + (i + 1) % peers) for i in range(count)]
    down = [(target, source) for source, target in up]
    seams = [(i, (i + peers) % count) for i in range(peers, count, peers)] + [(0, count - 1)]
    seams += [(i, i - peers) for i in range(2 * peers - 1, count, peers)] + [(peers - 1, peers)]
    before = lax.ppermute(here, axes, up)
    after = lax.ppermute(here, axes, down)
    mixed, shares, chosen = call(
        tables_kernel,
        (
            shape((16, half * LANES), F32),
            shape((16, LANES), F32),
            shape((16, entries * TILE), F32),
        ),
        [SMEM, VMEM, VMEM, VMEM],
        (VMEM,) * 3,
    )(entry_src, atm_state, atm_frac.reshape(atm_cells // LANES, LANES), couple)
    fluxes, back = call(
        merge_kernel,
        (shape((16, half * LANES), F32), shape((peers * 4, LANES), BF16)),
        [SMEM, VMEM, VMEM, VMEM],
        (VMEM, VMEM),
        [pltpu.VMEM((peers * pitch, LANES), F32)],
    )(heat_coef, got, mixed, shares)
    back, neighbours, tracer = lax.optimization_barrier((back, neighbours, tracer))
    returned = lax.all_to_all(
        back.reshape(peers, 2, 2, LANES), "blk", split_axis=0, concat_axis=0, tiled=True
    ).reshape(peers * 4, LANES)
    own, edge, base, depth, speed, rate = call(
        base_kernel,
        (
            shape((cells, cells), BF16),
            shape((2 * HALO, cells), BF16),
            shape((levels, cells), F32),
            shape((levels, LANES), F32),
            shape((levels, LANES), F32),
            shape((levels, LANES), F32),
        ),
        [SMEM, VMEM, VMEM, VMEM],
        (VMEM,) * 6,
        flops=1_000_000_000,
    )(kappa, neighbours, tracer, mask)
    heat, forced, halo = call(
        heat_kernel,
        (shape((1, cells), F32), shape((levels, LANES), F32), shape((1, LANES), F32)),
        [VMEM] * 7,
        (VMEM,) * 3,
        [pltpu.VMEM((peers * 4, LANES), F32)],
    )(returned, chosen, here, before, after, mask, depth)
    swapped = lax.ppermute(forced, axes, seams)
    part, fluxes = call(
        partial_kernel,
        (shape((levels, cells), F32), shape((rows, atm_cells), BF16)),
        [VMEM] * 7,
        (VMEM, VMEM),
        flops=100_000_000,
    )(heat, own, base, mask, depth, rate, fluxes)
    tracer_out = call(finish_kernel, shape((levels, cells), F32), [VMEM] * 8, VMEM)(
        halo, swapped, before, after, edge, part, speed, rate
    )
    return (fluxes, tracer_out)


def solution(mesh):
    split = ("grp", "blk")
    return jax.shard_map(
        shards,
        mesh=mesh,
        in_specs=(
            P(None, split),
            P(split),
            P(split),
            P(split, None),
            P(split),
            P(split, None),
            P(None, split),
            P(split),
            P(),
            P(),
            P(),
            P(None, split),
            P(None, split),
        ),
        out_specs=(P(None, split), P(None, split)),
        check_vma=False,
    )
```

```python
import jax
import jax.numpy as jnp
from jax import lax
from jax.experimental import pallas as pl
from jax.experimental.pallas import tpu as pltpu
from jax.sharding import PartitionSpec as P

TILE = 64
HALO = 64
LANES = 128
PITCH = 33
WIDE = 65
F32 = jnp.float32
BF16 = jnp.bfloat16
SMEM = pl.BlockSpec(memory_space=pltpu.SMEM)
VMEM = pl.BlockSpec(memory_space=pltpu.VMEM)
HBM = pl.BlockSpec(memory_space=pltpu.HBM)


def iota(shape, dim):
    return lax.broadcasted_iota(jnp.int32, shape, dim)


def parts(value, count):
    out = []
    for _ in range(count - 1):
        high = value.astype(BF16).astype(F32)
        out.append(high)
        value = value - high
    out.append(value)
    return jnp.concatenate(out, axis=0).astype(BF16)


def column(scalars, count, rows):
    where = iota((rows, LANES), 0)
    out = jnp.zeros((rows, LANES), F32)
    for i in range(count):
        out = jnp.where(where == i, scalars[i], out)
    return out


def mm(a, b):
    return jnp.dot(a, b, preferred_element_type=F32)


def line(block):
    return jnp.concatenate([block[i : i + 1, :] for i in range(block.shape[0])], axis=1)


def across(col, width):
    return jnp.concatenate([col] * (width // LANES), axis=1)


def pack_kernel(
    src_hbm, route_hbm, tile_hbm, fields_hbm, mask_hbm, couple_hbm, weights_hbm, out,
    src, route, tile, fields, mask, couple, weights, tiles, wide, slots, seen, sems,
):
    pairs = (
        (fields_hbm, fields),
        (mask_hbm, mask),
        (couple_hbm, couple),
        (route_hbm, route),
        (src_hbm, src),
        (tile_hbm, tile),
        (weights_hbm, weights),
    )
    copies = [pltpu.make_async_copy(a, b, sems.at[i]) for i, (a, b) in enumerate(pairs)]
    for copy in copies:
        copy.start()
    entries = weights.shape[0]
    rows = couple.shape[0]
    half = rows // 2
    slots[...] = jnp.zeros(slots.shape, F32)
    for copy in copies[:3]:
        copy.wait()
    mixed = mm(parts(couple[...], 3), fields[...])
    mixed = mixed[:rows] + mixed[rows : 2 * rows] + mixed[2 * rows :]
    mixed = mixed * line(mask[...].astype(F32))
    high = mixed.astype(BF16).astype(F32)
    low = mixed - high
    flip = lambda x: jnp.concatenate([x[half:], x[:half]], axis=0)
    straight = jnp.concatenate([high, low], axis=0)
    swapped = jnp.concatenate([flip(high), flip(low)], axis=0)
    count = mixed.shape[1] // LANES
    stacks = [
        jnp.concatenate([x[:, j * LANES : (j + 1) * LANES] for j in range(count)], axis=0).astype(BF16)
        for x in (straight, swapped)
    ]
    for k in range(4):
        wanted = iota((LANES, TILE // 2), 1) * 2 + ((k // 2) * TILE + k % 2)
        pick = (iota((LANES, TILE // 2), 0) == wanted).astype(F32).astype(BF16)
        part = mm(stacks[k % 2], pick).astype(BF16)
        at = (k % 2) * 2 * rows
        for j in range(count):
            tiles[2 * j + k // 2, at : at + 2 * rows, :] = part[2 * rows * j : 2 * rows * (j + 1)]
    for copy in copies[3:]:
        copy.wait()
    for e in range(entries):
        seen[route[e]] = 0
    flat = weights[...].astype(F32)
    for g in range(entries // 8):
        for j in range(TILE // 2):
            wide[pl.ds(g * 8 * PITCH + j, 8, stride=PITCH), :] = flat[
                g * 8 : (g + 1) * 8, j * LANES : (j + 1) * LANES
            ]
    left = iota((rows, LANES), 1) < TILE
    for e in range(entries):
        to = route[e]
        rank = seen[to]
        seen[to] = rank + 1
        at = (to * 2 + rank) * (half + 1)
        sent = mm(tiles[src[e]], wide[e * PITCH : e * PITCH + TILE // 2, :].astype(BF16))
        even = sent[:rows] + sent[rows : 2 * rows]
        odd = sent[2 * rows : 3 * rows] + sent[3 * rows :]
        both = jnp.where(left, even, odd)
        slots[pl.ds(at, half), :] = both[:half] + pltpu.roll(both, TILE, 1)[half:]
        slots[pl.ds(at + half, 1), :] = jnp.full((1, LANES), tile[e] + 1, jnp.int32).astype(F32)
    out[...] = slots[...].astype(BF16)


def ship_kernel(src, route, weights, tracer, mask, out, seen, wide):
    entries = src.shape[0]
    levels, cells = tracer.shape
    half = entries * TILE // 2
    for e in range(entries):
        seen[route[e]] = 0
    slots = []
    for e in range(entries):
        to = route[e]
        rank = seen[to]
        seen[to] = rank + 1
        slots.append(to * 2 + rank)
    flat = weights[...].astype(F32)
    low = iota((8, LANES), 1) < TILE
    for g in range(entries // 8):
        for j in range(TILE // 2):
            block = flat[g * 8 : (g + 1) * 8, j * LANES : (j + 1) * LANES]
            at = g * 8 * WIDE + 2 * j
            wide[pl.ds(at, 8, stride=WIDE), :] = jnp.where(low, block, 0.0)
            wide[pl.ds(at + 1, 8, stride=WIDE), :] = jnp.where(low, 0.0, block)
    eye = iota((TILE, LANES), 0) == (iota((TILE, LANES), 1) & (TILE - 1))
    eye = eye.astype(F32).astype(BF16)
    for e in range(entries // 2):
        pair = [wide[i * WIDE : i * WIDE + TILE, :] for i in (e, e + entries // 2)]
        rows = jnp.concatenate(pair, axis=0).astype(BF16)
        turned = lax.dot_general(eye, rows, (((1,), (1,)), ((), ())), preferred_element_type=F32)
        out[e * TILE : (e + 1) * TILE, :] = turned.astype(BF16)
    ends = lambda x: jnp.concatenate([x[:, cells - HALO :], x[:, :HALO]], axis=1)
    sea = ends(line(mask[...].astype(F32)))
    edge = ends(tracer[...]) * sea
    out[half : half + 32, :] = jnp.concatenate(
        [edge, jnp.broadcast_to(sea, (32 - levels, LANES))], axis=0
    ).astype(BF16)
    where = iota((32, LANES), 0)
    slot_rows = jnp.full((32, LANES), -1, jnp.int32)
    tile_rows = jnp.full((32, LANES), -1, jnp.int32)
    for e in range(entries):
        here = where == (e // 2 + 16 * (e % 2))
        slot_rows = jnp.where(here, slots[e], slot_rows)
        tile_rows = jnp.where(here, src[e], tile_rows)
    out[half + 32 : half + 64, :] = slot_rows.astype(F32).astype(BF16)
    out[half + 64 : half + 96, :] = tile_rows.astype(F32).astype(BF16)


def tables_kernel(src, state, frac, couple, mixed, shares, chosen):
    entries = src.shape[0]
    rows = couple.shape[0]
    half = rows // 2
    part = mm(parts(couple[...], 3), state[...])
    part = part[:rows] + part[rows : 2 * rows] + part[2 * rows :]
    mixed[...] = jnp.zeros(mixed.shape, F32)
    shares[...] = jnp.zeros(shares.shape, F32)
    low = iota((half, LANES), 1) < TILE
    for i in range(state.shape[1] // LANES):
        here = part[:, i * LANES : (i + 1) * LANES]
        there = pltpu.roll(here, TILE, 1)
        one = jnp.where(low, here[:half], there[half:])
        two = jnp.where(low, there[:half], here[half:])
        for q in range(half):
            at = slice(q * LANES, (q + 1) * LANES)
            mixed[2 * i : 2 * i + 1, at] = one[q : q + 1]
            mixed[2 * i + 1 : 2 * i + 2, at] = two[q : q + 1]
        here = frac[i : i + 1, :]
        there = pltpu.roll(here, TILE, 1)
        shares[2 * i : 2 * i + 1, :] = jnp.where(low[:1], here, there)
        shares[2 * i + 1 : 2 * i + 2, :] = jnp.where(low[:1], there, here)

    low = iota((16, LANES), 1) < TILE
    for j in range(entries // 2):
        owner = jnp.where(low, src[2 * j], src[2 * j + 1])
        chosen[:, j * LANES : (j + 1) * LANES] = (iota((16, LANES), 0) == owner).astype(F32)


def merge_kernel(heat_coef, got, mixed, shares, fluxes, back, flat):
    half = mixed.shape[1] // LANES
    peers = back.shape[0] // 4
    pitch = 2 * (half + 1)
    flat[...] = got[...].astype(F32)
    row = lambda rank, q: flat[pl.ds(rank * (half + 1) + q, peers, stride=pitch), :]
    first, second = row(0, half), row(1, half)
    named = jnp.concatenate([first, second], axis=0).astype(BF16)
    pick = (iota((16, LANES), 1) == 0).astype(F32).astype(BF16)
    ids = lax.dot_general(pick, named, (((1,), (1,)), ((), ())), preferred_element_type=F32)
    member = (ids == (iota(ids.shape, 0) + 1).astype(F32)).astype(F32).astype(BF16)
    values = jnp.concatenate(
        [jnp.concatenate([row(0, q), row(1, q)], axis=0) for q in range(half)], axis=1
    ).astype(BF16)
    remap = mm(member, values)
    low = iota((1, LANES), 1) < TILE
    heat = jnp.zeros((16, LANES), F32)
    for q in range(half):
        at = slice(q * LANES, (q + 1) * LANES)
        flux = ((mixed[:, at] - remap[:, at]) * shares[...]).astype(BF16).astype(F32)
        fluxes[:, at] = flux
        heat = heat + flux * jnp.where(low, heat_coef[q], heat_coef[q + half])
    heat = heat + pltpu.roll(heat, TILE, 1)
    high = heat.astype(BF16).astype(F32)
    heat = jnp.concatenate([high, heat - high], axis=0)
    blank = jnp.zeros((32, LANES), F32)
    spread = jnp.concatenate(
        [jnp.where(low, heat, 0.0), blank, jnp.where(low, 0.0, heat), blank], axis=0
    ).astype(BF16)
    lane = iota((peers, LANES), 1)
    target = jnp.where((lane & (TILE - 1)) < 32, (lane & 15) + 1, -1).astype(F32)
    asked = jnp.where(lane < TILE, first, second)
    reply = mm((asked == target).astype(F32).astype(BF16), spread)
    high = reply.astype(BF16).astype(F32)
    four = (high, reply - high, pltpu.roll(high, 1, 0), pltpu.roll(high, peers - 1, 0))
    for k, rows in enumerate(four):
        flat[pl.ds(k, peers, stride=4), :] = rows
    back[...] = flat[: 4 * peers, :].astype(BF16)


def base_kernel(kappa, near, tracer, mask, own, edge, base, depth, speed, rate):
    levels, cells = tracer.shape
    place = iota((LANES, cells), 0).astype(F32).astype(BF16)

    def counts(start):
        total = jnp.zeros(place.shape, BF16)
        for k in range(near.shape[0]):
            at = jnp.clip(near[k : k + 1, :] - start, -1, LANES).astype(F32).astype(BF16)
            total = total + jnp.where(at == place, jnp.ones((), BF16), jnp.zeros((), BF16))
        return total

    @pl.loop(0, cells // LANES)
    def _(i):
        at = pl.multiple_of(i * LANES, LANES)
        own[pl.ds(at, LANES), :] = counts(at + HALO)

    sea = line(mask[...].astype(F32))
    land = sea.astype(BF16)
    edge[:HALO, :] = (land * counts(0))[:HALO]
    edge[HALO:, :] = (land * counts(cells + HALO))[:HALO]

    value = tracer[...]
    pad = jnp.zeros((32 - levels, cells), F32)
    total = mm(parts(jnp.concatenate([value * sea, pad], axis=0), 2), own[...])
    total = sea * ((total[:32] + total[32:])[:levels] - 6.0 * value)
    pace = column(kappa, levels, levels)
    deep = jnp.exp(-iota((levels, LANES), 0).astype(F32) / 10.0)
    depth[...] = deep
    speed[...] = pace
    rate[...] = deep * pace
    base[...] = value + across(pace, cells) * total


def in_group(shape):
    me = lax.axis_index("blk")
    low = iota(shape, 1) < TILE
    return jnp.where(low, me, lax.axis_size("blk") - 1 - me) > 0


def heat_kernel(got, chosen, here, before, after, mask, depth, heat, forced, ends, halo, flat):
    cells = heat.shape[1]
    half = here.shape[0] - 96
    lane = iota((32, LANES), 1)
    target = ((lane & (TILE - 1)) * 2 + (lane >> 6)).astype(F32)
    meta = lambda ref, at: ref[half + at : half + at + 32, :].astype(F32)
    found = lambda ref: meta(ref, 32) == target
    last = float(cells // TILE - 1)
    picks = [
        pick.astype(F32).astype(BF16)
        for pick in (
            found(here),
            found(before) & (meta(before, 64) == last),
            found(after) & (meta(after, 64) == 0.0),
        )
    ]
    peers = got.shape[0] // 4
    count = half // LANES
    flat[...] = got[...].astype(F32)
    low = iota((16, LANES), 1) < TILE

    def lookup(k, which):
        rows = flat[pl.ds(k, peers, stride=4), :]
        turned = pltpu.roll(rows, TILE, 1)
        one = jnp.concatenate([rows, turned], axis=0).astype(BF16)
        two = jnp.concatenate([turned, rows], axis=0).astype(BF16)
        return jnp.where(low, mm(picks[which][:16], one), mm(picks[which][16:], two))

    def laid(rows, start):
        return jnp.concatenate([rows[j : j + 1] for j in range(start, start + count)], axis=1)

    high, rest = lookup(0, 0), lookup(1, 0)
    previous, following = lookup(2, 1), lookup(3, 2)
    spread = []
    for h in range(2):
        pick = chosen[:, h * half : (h + 1) * half]
        for rows in (high, rest):
            spread.append(pick * laid(rows, h * count))
    summed = mm(jnp.concatenate(spread, axis=0).astype(BF16), here[:half, :])
    summed = summed[:16] + summed[16:32] + pltpu.roll(summed[32:48] + summed[48:], TILE, 1)
    blank = jnp.zeros((14, half), F32)

    def side(rows, ref):
        rows = jnp.concatenate([laid(rows, 0), laid(rows, count), blank], axis=0)
        return mm(rows.astype(BF16), ref[:half, :])

    left, right = side(previous, before), side(following, after)
    left = left[0:1] + pltpu.roll(left, TILE, 1)[1:2]
    right = right[1:2] + pltpu.roll(right, TILE, 1)[0:1]
    levels = depth.shape[0]
    coast = jnp.where(low[:1], meta(before, 0)[levels : levels + 1], meta(after, 0)[levels : levels + 1])
    beside = jnp.where(low[:1], left, right) * coast
    halo[...] = beside
    edges = jnp.where(lane < TILE, meta(before, 0), meta(after, 0))[:levels]
    deep = depth[...]
    forced[...] = edges + deep * beside
    row = jnp.concatenate([summed[t : t + 1, :TILE] for t in range(cells // TILE)], axis=1)
    row = row * line(mask[...].astype(F32))
    heat[...] = row
    edge = jnp.concatenate([row[:, cells - HALO :], row[:, :HALO]], axis=1)
    ends[...] = meta(here, 0)[:levels] + deep * edge


def halves(row):
    high = row.astype(BF16).astype(F32)
    blank = jnp.zeros((14, row.shape[1]), F32)
    return jnp.concatenate([high, row - high, blank], axis=0).astype(BF16)


def partial_kernel(heat, own, base, mask, depth, rate, fluxes, out, placed):
    half = placed.shape[0] // 2
    low = iota((half, LANES), 1) < TILE
    for i in range(placed.shape[1] // LANES):
        piece = lambda t: jnp.concatenate(
            [fluxes[t : t + 1, q * LANES : (q + 1) * LANES] for q in range(half)], axis=0
        )
        one, two = piece(2 * i), piece(2 * i + 1)
        block = jnp.concatenate(
            [
                jnp.where(low, one, pltpu.roll(two, TILE, 1)),
                jnp.where(low, pltpu.roll(one, TILE, 1), two),
            ],
            axis=0,
        )
        placed[:, i * LANES : (i + 1) * LANES] = block.astype(BF16)
    cells = base.shape[1]
    sea = line(mask[...].astype(F32))
    row = heat[...]
    near = mm(halves(row), own[...])
    near = sea * (near[0:1] + near[1:2] - 6.0 * row)
    out[...] = base[...] + across(depth[...], cells) * row + across(rate[...], cells) * near


def finish_kernel(halo, swapped, closing, before, after, edge, part, speed, rate, out):
    levels, cells = part.shape
    first = before.shape[0] - 96
    rows = slice(first, first + 32)
    low = iota((32, LANES), 1) < TILE
    outer = jnp.where(low, before[rows, :].astype(F32), after[rows, :].astype(F32))[:levels]
    outer = jnp.where(in_group((levels, LANES)), outer, swapped[...] + closing[...]) * speed[...]
    pad = jnp.zeros((32 - levels, LANES), F32)
    outer = parts(jnp.concatenate([outer, pad], axis=0), 2)
    inner = halves(jnp.where(in_group((1, LANES)), halo[...], 0.0))
    near = mm(jnp.concatenate([outer, inner], axis=0), edge[...])
    inner = near[64:65] + near[65:66]
    out[...] = part[...] + (near[:32] + near[32:64])[:levels] + across(rate[...], cells) * inner


def call(kernel, out_shape, in_specs, out_specs, scratch=(), flops=2_000_000_000, vmem=24 * 2**20):
    return pl.pallas_call(
        kernel,
        out_shape=out_shape,
        in_specs=in_specs,
        out_specs=out_specs,
        scratch_shapes=list(scratch),
        cost_estimate=pl.CostEstimate(flops=flops, bytes_accessed=30_000_000, transcendentals=0),
        compiler_params=pltpu.CompilerParams(vmem_limit_bytes=vmem),
    )


def in_hbm(array):
    return pltpu.with_memory_space_constraint(array, pltpu.HBM)


def shards(
    ocean_fields,
    ocean_mask,
    entry_src,
    entry_route,
    entry_tile,
    weight_tiles,
    atm_state,
    atm_frac,
    couple,
    heat_coef,
    kappa,
    tracer,
    neighbours,
):
    fields, cells = ocean_fields.shape
    entries = entry_src.shape[0]
    atm_cells = atm_state.shape[1]
    rows = couple.shape[0]
    levels = tracer.shape[0]
    peers = lax.axis_size("blk")
    shape = jax.ShapeDtypeStruct
    half = rows // 2
    mask = ocean_mask.reshape(cells // LANES, LANES)
    route = entry_route.reshape(entries)
    pitch = 2 * (half + 1)
    i32 = jnp.int32
    sent = call(
        pack_kernel,
        shape((peers * pitch, LANES), BF16),
        [HBM] * 7,
        VMEM,
        [
            pltpu.SMEM((entries,), i32),
            pltpu.SMEM((entries,), i32),
            pltpu.SMEM((entries,), i32),
            pltpu.VMEM((fields, cells), BF16),
            pltpu.VMEM((cells // LANES, LANES), i32),
            pltpu.VMEM((rows, fields), F32),
            pltpu.VMEM((entries, TILE * TILE), BF16),
            pltpu.VMEM((cells // TILE, 4 * rows, TILE // 2), BF16),
            pltpu.VMEM((entries * PITCH, LANES), F32),
            pltpu.VMEM((peers * pitch, LANES), F32),
            pltpu.SMEM((peers,), i32),
            pltpu.SemaphoreType.DMA((7,)),
        ],
        vmem=64 * 2**20,
    )(entry_src, route, entry_tile, ocean_fields, mask, couple, weight_tiles)
    sent, weight_tiles, neighbours, atm_state, tracer = lax.optimization_barrier(
        (sent, weight_tiles, neighbours, atm_state, tracer)
    )
    got = lax.all_to_all(
        sent.reshape(peers, half + 1, 2, LANES), "blk", split_axis=0, concat_axis=0, tiled=True
    ).reshape(peers * pitch, LANES)
    here = call(
        ship_kernel,
        shape((entries * TILE // 2 + 96, LANES), BF16),
        [SMEM, SMEM, VMEM, VMEM, VMEM],
        VMEM,
        [pltpu.SMEM((peers,), i32), pltpu.VMEM((entries * WIDE, LANES), F32)],
    )(*(in_hbm(x) for x in (entry_src, route, weight_tiles, tracer, mask)))
    axes = ("grp", "blk")
    count = lax.axis_size(axes)
    up = [(i, i - i % peers + (i + 1) % peers) for i in range(count)]
    down = [(target, source) for source, target in up]
    seams = [(i, (i + peers) % count) for i in range(0, count, peers)]
    seams += [(i, i - peers) for i in range(2 * peers - 1, count, peers)]
    before = lax.ppermute(here, axes, up)
    after = lax.ppermute(here, axes, down)
    mixed, shares, chosen = call(
        tables_kernel,
        (
            shape((16, half * LANES), F32),
            shape((16, LANES), F32),
            shape((16, entries * TILE), F32),
        ),
        [SMEM, VMEM, VMEM, VMEM],
        (VMEM,) * 3,
    )(entry_src, atm_state, atm_frac.reshape(atm_cells // LANES, LANES), couple)
    fluxes, back = call(
        merge_kernel,
        (shape((16, half * LANES), F32), shape((peers * 4, LANES), BF16)),
        [SMEM, VMEM, VMEM, VMEM],
        (VMEM, VMEM),
        [pltpu.VMEM((peers * pitch, LANES), F32)],
    )(heat_coef, got, mixed, shares)
    back, neighbours, tracer = lax.optimization_barrier((back, neighbours, tracer))
    returned = lax.all_to_all(
        back.reshape(peers, 2, 2, LANES), "blk", split_axis=0, concat_axis=0, tiled=True
    ).reshape(peers * 4, LANES)
    own, edge, base, depth, speed, rate = call(
        base_kernel,
        (
            shape((cells, cells), BF16),
            shape((2 * HALO, cells), BF16),
            shape((levels, cells), F32),
            shape((levels, LANES), F32),
            shape((levels, LANES), F32),
            shape((levels, LANES), F32),
        ),
        [SMEM, VMEM, VMEM, VMEM],
        (VMEM,) * 6,
        flops=1_000_000_000,
    )(kappa, neighbours, tracer, mask)
    heat, forced, ends, halo = call(
        heat_kernel,
        (
            shape((1, cells), F32),
            shape((levels, LANES), F32),
            shape((levels, LANES), F32),
            shape((1, LANES), F32),
        ),
        [VMEM] * 7,
        (VMEM,) * 4,
        [pltpu.VMEM((peers * 4, LANES), F32)],
    )(returned, chosen, here, before, after, mask, depth)
    swapped = lax.ppermute(forced, axes, seams)
    closing = lax.ppermute(ends, axes, [(0, count - 1)])
    part, fluxes = call(
        partial_kernel,
        (shape((levels, cells), F32), shape((rows, atm_cells), BF16)),
        [VMEM] * 7,
        (VMEM, VMEM),
        flops=100_000_000,
    )(heat, own, base, mask, depth, rate, fluxes)
    tracer_out = call(finish_kernel, shape((levels, cells), F32), [VMEM] * 9, VMEM)(
        halo, swapped, closing, before, after, edge, part, speed, rate
    )
    return (fluxes, tracer_out)


def solution(mesh):
    split = ("grp", "blk")
    return jax.shard_map(
        shards,
        mesh=mesh,
        in_specs=(
            P(None, split),
            P(split),
            P(split),
            P(split, None),
            P(split),
            P(split, None),
            P(None, split),
            P(split),
            P(),
            P(),
            P(),
            P(None, split),
            P(None, split),
        ),
        out_specs=(P(None, split), P(None, split)),
        check_vma=False,
    )
```

```python
import jax
import jax.numpy as jnp
from jax import lax
from jax.experimental import pallas as pl
from jax.experimental.pallas import tpu as pltpu
from jax.sharding import PartitionSpec as P

TILE = 64
HALO = 64
LANES = 128
PITCH = 33
WIDE = 65
F32 = jnp.float32
BF16 = jnp.bfloat16
SMEM = pl.BlockSpec(memory_space=pltpu.SMEM)
VMEM = pl.BlockSpec(memory_space=pltpu.VMEM)
HBM = pl.BlockSpec(memory_space=pltpu.HBM)


def iota(shape, dim):
    return lax.broadcasted_iota(jnp.int32, shape, dim)


def parts(value, count):
    out = []
    for _ in range(count - 1):
        high = value.astype(BF16).astype(F32)
        out.append(high)
        value = value - high
    out.append(value)
    return jnp.concatenate(out, axis=0).astype(BF16)


def column(scalars, count, rows):
    where = iota((rows, LANES), 0)
    out = jnp.zeros((rows, LANES), F32)
    for i in range(count):
        out = jnp.where(where == i, scalars[i], out)
    return out


def mm(a, b):
    return jnp.dot(a, b, preferred_element_type=F32)


def line(block):
    return jnp.concatenate([block[i : i + 1, :] for i in range(block.shape[0])], axis=1)


def across(col, width):
    return jnp.concatenate([col] * (width // LANES), axis=1)


def pack_kernel(
    src_hbm, route_hbm, tile_hbm, fields_hbm, mask_hbm, couple_hbm, weights_hbm, out,
    src, route, tile, fields, mask, couple, weights, tiles, wide, slots, seen, sems,
):
    pairs = (
        (fields_hbm, fields),
        (mask_hbm, mask),
        (couple_hbm, couple),
        (route_hbm, route),
        (src_hbm, src),
        (tile_hbm, tile),
        (weights_hbm, weights),
    )
    copies = [pltpu.make_async_copy(a, b, sems.at[i]) for i, (a, b) in enumerate(pairs)]
    for copy in copies:
        copy.start()
    entries = weights.shape[0]
    rows = couple.shape[0]
    half = rows // 2
    slots[...] = jnp.zeros(slots.shape, F32)
    for copy in copies[:3]:
        copy.wait()
    mixed = mm(parts(couple[...], 3), fields[...])
    mixed = mixed[:rows] + mixed[rows : 2 * rows] + mixed[2 * rows :]
    mixed = mixed * line(mask[...].astype(F32))
    high = mixed.astype(BF16).astype(F32)
    low = mixed - high
    flip = lambda x: jnp.concatenate([x[half:], x[:half]], axis=0)
    straight = jnp.concatenate([high, low], axis=0)
    swapped = jnp.concatenate([flip(high), flip(low)], axis=0)
    count = mixed.shape[1] // LANES
    stacks = [
        jnp.concatenate([x[:, j * LANES : (j + 1) * LANES] for j in range(count)], axis=0).astype(BF16)
        for x in (straight, swapped)
    ]
    for k in range(4):
        wanted = iota((LANES, TILE // 2), 1) * 2 + ((k // 2) * TILE + k % 2)
        pick = (iota((LANES, TILE // 2), 0) == wanted).astype(F32).astype(BF16)
        part = mm(stacks[k % 2], pick).astype(BF16)
        at = (k % 2) * 2 * rows
        for j in range(count):
            tiles[2 * j + k // 2, at : at + 2 * rows, :] = part[2 * rows * j : 2 * rows * (j + 1)]
    for copy in copies[3:]:
        copy.wait()
    for e in range(entries):
        seen[route[e]] = 0
    flat = weights[...].astype(F32)
    for g in range(entries // 8):
        for j in range(TILE // 2):
            wide[pl.ds(g * 8 * PITCH + j, 8, stride=PITCH), :] = flat[
                g * 8 : (g + 1) * 8, j * LANES : (j + 1) * LANES
            ]
    left = iota((rows, LANES), 1) < TILE
    for e in range(entries):
        to = route[e]
        rank = seen[to]
        seen[to] = rank + 1
        at = (to * 2 + rank) * (half + 1)
        sent = mm(tiles[src[e]], wide[e * PITCH : e * PITCH + TILE // 2, :].astype(BF16))
        even = sent[:rows] + sent[rows : 2 * rows]
        odd = sent[2 * rows : 3 * rows] + sent[3 * rows :]
        both = jnp.where(left, even, odd)
        slots[pl.ds(at, half), :] = both[:half] + pltpu.roll(both, TILE, 1)[half:]
        slots[pl.ds(at + half, 1), :] = jnp.full((1, LANES), tile[e] + 1, jnp.int32).astype(F32)
    out[...] = slots[: out.shape[0], :].astype(BF16)


def ship_kernel(src, route, weights, tracer, mask, out, seen, wide):
    entries = src.shape[0]
    levels, cells = tracer.shape
    half = entries * TILE // 2
    for e in range(entries):
        seen[route[e]] = 0
    slots = []
    for e in range(entries):
        to = route[e]
        rank = seen[to]
        seen[to] = rank + 1
        slots.append(to * 2 + rank)
    flat = weights[...].astype(F32)
    low = iota((8, LANES), 1) < TILE
    for g in range(entries // 8):
        for j in range(TILE // 2):
            block = flat[g * 8 : (g + 1) * 8, j * LANES : (j + 1) * LANES]
            at = g * 8 * WIDE + 2 * j
            wide[pl.ds(at, 8, stride=WIDE), :] = jnp.where(low, block, 0.0)
            wide[pl.ds(at + 1, 8, stride=WIDE), :] = jnp.where(low, 0.0, block)
    eye = iota((TILE, LANES), 0) == (iota((TILE, LANES), 1) & (TILE - 1))
    eye = eye.astype(F32).astype(BF16)
    for e in range(entries // 2):
        pair = [wide[i * WIDE : i * WIDE + TILE, :] for i in (e, e + entries // 2)]
        rows = jnp.concatenate(pair, axis=0).astype(BF16)
        turned = lax.dot_general(eye, rows, (((1,), (1,)), ((), ())), preferred_element_type=F32)
        out[e * TILE : (e + 1) * TILE, :] = turned.astype(BF16)
    ends = lambda x: jnp.concatenate([x[:, cells - HALO :], x[:, :HALO]], axis=1)
    sea = ends(line(mask[...].astype(F32)))
    edge = ends(tracer[...]) * sea
    out[half : half + 32, :] = jnp.concatenate(
        [edge, jnp.broadcast_to(sea, (32 - levels, LANES))], axis=0
    ).astype(BF16)
    where = iota((32, LANES), 0)
    slot_rows = jnp.full((32, LANES), -1, jnp.int32)
    tile_rows = jnp.full((32, LANES), -1, jnp.int32)
    for e in range(entries):
        here = where == (e // 2 + 16 * (e % 2))
        slot_rows = jnp.where(here, slots[e], slot_rows)
        tile_rows = jnp.where(here, src[e], tile_rows)
    out[half + 32 : half + 64, :] = slot_rows.astype(F32).astype(BF16)
    out[half + 64 : half + 96, :] = tile_rows.astype(F32).astype(BF16)


def tables_kernel(src, state, frac, couple, mixed, shares, chosen):
    entries = src.shape[0]
    rows = couple.shape[0]
    half = rows // 2
    part = mm(parts(couple[...], 3), state[...])
    part = part[:rows] + part[rows : 2 * rows] + part[2 * rows :]
    mixed[...] = jnp.zeros(mixed.shape, F32)
    shares[...] = jnp.zeros(shares.shape, F32)
    low = iota((half, LANES), 1) < TILE
    for i in range(state.shape[1] // LANES):
        here = part[:, i * LANES : (i + 1) * LANES]
        there = pltpu.roll(here, TILE, 1)
        one = jnp.where(low, here[:half], there[half:])
        two = jnp.where(low, there[:half], here[half:])
        for q in range(half):
            at = slice(q * LANES, (q + 1) * LANES)
            mixed[2 * i : 2 * i + 1, at] = one[q : q + 1]
            mixed[2 * i + 1 : 2 * i + 2, at] = two[q : q + 1]
        here = frac[i : i + 1, :]
        there = pltpu.roll(here, TILE, 1)
        shares[2 * i : 2 * i + 1, :] = jnp.where(low[:1], here, there)
        shares[2 * i + 1 : 2 * i + 2, :] = jnp.where(low[:1], there, here)

    low = iota((16, LANES), 1) < TILE
    for j in range(entries // 2):
        owner = jnp.where(low, src[2 * j], src[2 * j + 1])
        chosen[:, j * LANES : (j + 1) * LANES] = (iota((16, LANES), 0) == owner).astype(F32)


def merge_kernel(heat_coef, got, mixed, shares, fluxes, back, flat):
    half = mixed.shape[1] // LANES
    peers = back.shape[0] // 4
    pitch = 2 * (half + 1)
    flat[: got.shape[0], :] = got[...].astype(F32)
    row = lambda rank, q: flat[pl.ds(rank * (half + 1) + q, peers, stride=pitch), :]
    first, second = row(0, half), row(1, half)
    named = jnp.concatenate([first, second], axis=0).astype(BF16)
    pick = (iota((16, LANES), 1) == 0).astype(F32).astype(BF16)
    ids = lax.dot_general(pick, named, (((1,), (1,)), ((), ())), preferred_element_type=F32)
    member = (ids == (iota(ids.shape, 0) + 1).astype(F32)).astype(F32).astype(BF16)
    values = jnp.concatenate(
        [jnp.concatenate([row(0, q), row(1, q)], axis=0) for q in range(half)], axis=1
    ).astype(BF16)
    remap = mm(member, values)
    low = iota((1, LANES), 1) < TILE
    heat = jnp.zeros((16, LANES), F32)
    for q in range(half):
        at = slice(q * LANES, (q + 1) * LANES)
        flux = ((mixed[:, at] - remap[:, at]) * shares[...]).astype(BF16).astype(F32)
        fluxes[:, at] = flux
        heat = heat + flux * jnp.where(low, heat_coef[q], heat_coef[q + half])
    heat = heat + pltpu.roll(heat, TILE, 1)
    high = heat.astype(BF16).astype(F32)
    heat = jnp.concatenate([high, heat - high], axis=0)
    blank = jnp.zeros((32, LANES), F32)
    spread = jnp.concatenate(
        [jnp.where(low, heat, 0.0), blank, jnp.where(low, 0.0, heat), blank], axis=0
    ).astype(BF16)
    lane = iota((peers, LANES), 1)
    target = jnp.where((lane & (TILE - 1)) < 32, (lane & 15) + 1, -1).astype(F32)
    asked = jnp.where(lane < TILE, first, second)
    reply = mm((asked == target).astype(F32).astype(BF16), spread)
    high = reply.astype(BF16).astype(F32)
    four = (high, reply - high, pltpu.roll(high, 1, 0), pltpu.roll(high, peers - 1, 0))
    for k, rows in enumerate(four):
        flat[pl.ds(k, peers, stride=4), :] = rows
    back[...] = flat[: 4 * peers, :].astype(BF16)


def base_kernel(kappa, near, tracer, mask, own, edge, base, depth, speed, rate):
    levels, cells = tracer.shape
    place = iota((LANES, cells), 0).astype(F32).astype(BF16)

    def counts(start):
        total = jnp.zeros(place.shape, BF16)
        for k in range(near.shape[0]):
            at = jnp.clip(near[k : k + 1, :] - start, -1, LANES).astype(F32).astype(BF16)
            total = total + jnp.where(at == place, jnp.ones((), BF16), jnp.zeros((), BF16))
        return total

    @pl.loop(0, cells // LANES)
    def _(i):
        at = pl.multiple_of(i * LANES, LANES)
        own[pl.ds(at, LANES), :] = counts(at + HALO)

    sea = line(mask[...].astype(F32))
    land = sea.astype(BF16)
    edge[:HALO, :] = (land * counts(0))[:HALO]
    edge[HALO:, :] = (land * counts(cells + HALO))[:HALO]

    value = tracer[...]
    pad = jnp.zeros((32 - levels, cells), F32)
    total = mm(parts(jnp.concatenate([value * sea, pad], axis=0), 2), own[...])
    total = sea * ((total[:32] + total[32:])[:levels] - 6.0 * value)
    pace = column(kappa, levels, levels)
    deep = jnp.exp(-iota((levels, LANES), 0).astype(F32) / 10.0)
    depth[...] = deep
    speed[...] = pace
    rate[...] = deep * pace
    base[...] = value + across(pace, cells) * total


def in_group(shape):
    me = lax.axis_index("blk")
    low = iota(shape, 1) < TILE
    return jnp.where(low, me, lax.axis_size("blk") - 1 - me) > 0


def heat_kernel(got, chosen, here, before, after, mask, depth, heat, forced, ends, halo, flat):
    cells = heat.shape[1]
    half = here.shape[0] - 96
    lane = iota((32, LANES), 1)
    target = ((lane & (TILE - 1)) * 2 + (lane >> 6)).astype(F32)
    meta = lambda ref, at: ref[half + at : half + at + 32, :].astype(F32)
    found = lambda ref: meta(ref, 32) == target
    last = float(cells // TILE - 1)
    picks = [
        pick.astype(F32).astype(BF16)
        for pick in (
            found(here),
            found(before) & (meta(before, 64) == last),
            found(after) & (meta(after, 64) == 0.0),
        )
    ]
    peers = got.shape[0] // 4
    count = half // LANES
    flat[: got.shape[0], :] = got[...].astype(F32)
    low = iota((16, LANES), 1) < TILE

    def lookup(k, which):
        rows = flat[pl.ds(k, peers, stride=4), :]
        turned = pltpu.roll(rows, TILE, 1)
        one = jnp.concatenate([rows, turned], axis=0).astype(BF16)
        two = jnp.concatenate([turned, rows], axis=0).astype(BF16)
        return jnp.where(low, mm(picks[which][:16], one), mm(picks[which][16:], two))

    def laid(rows, start):
        return jnp.concatenate([rows[j : j + 1] for j in range(start, start + count)], axis=1)

    high, rest = lookup(0, 0), lookup(1, 0)
    previous, following = lookup(2, 1), lookup(3, 2)
    spread = []
    for h in range(2):
        pick = chosen[:, h * half : (h + 1) * half]
        for rows in (high, rest):
            spread.append(pick * laid(rows, h * count))
    summed = mm(jnp.concatenate(spread, axis=0).astype(BF16), here[:half, :])
    summed = summed[:16] + summed[16:32] + pltpu.roll(summed[32:48] + summed[48:], TILE, 1)
    blank = jnp.zeros((14, half), F32)

    def side(rows, ref):
        rows = jnp.concatenate([laid(rows, 0), laid(rows, count), blank], axis=0)
        return mm(rows.astype(BF16), ref[:half, :])

    left, right = side(previous, before), side(following, after)
    left = left[0:1] + pltpu.roll(left, TILE, 1)[1:2]
    right = right[1:2] + pltpu.roll(right, TILE, 1)[0:1]
    levels = depth.shape[0]
    coast = jnp.where(low[:1], meta(before, 0)[levels : levels + 1], meta(after, 0)[levels : levels + 1])
    beside = jnp.where(low[:1], left, right) * coast
    halo[...] = beside
    edges = jnp.where(lane < TILE, meta(before, 0), meta(after, 0))[:levels]
    deep = depth[...]
    forced[...] = edges + deep * beside
    row = jnp.concatenate([summed[t : t + 1, :TILE] for t in range(cells // TILE)], axis=1)
    row = row * line(mask[...].astype(F32))
    heat[...] = row
    edge = jnp.concatenate([row[:, cells - HALO :], row[:, :HALO]], axis=1)
    ends[...] = meta(here, 0)[:levels] + deep * edge


def halves(row):
    high = row.astype(BF16).astype(F32)
    blank = jnp.zeros((14, row.shape[1]), F32)
    return jnp.concatenate([high, row - high, blank], axis=0).astype(BF16)


def partial_kernel(heat, own, base, mask, depth, rate, fluxes, out, placed):
    half = placed.shape[0] // 2
    low = iota((half, LANES), 1) < TILE
    for i in range(placed.shape[1] // LANES):
        piece = lambda t: jnp.concatenate(
            [fluxes[t : t + 1, q * LANES : (q + 1) * LANES] for q in range(half)], axis=0
        )
        one, two = piece(2 * i), piece(2 * i + 1)
        block = jnp.concatenate(
            [
                jnp.where(low, one, pltpu.roll(two, TILE, 1)),
                jnp.where(low, pltpu.roll(one, TILE, 1), two),
            ],
            axis=0,
        )
        placed[:, i * LANES : (i + 1) * LANES] = block.astype(BF16)
    cells = base.shape[1]
    sea = line(mask[...].astype(F32))
    row = heat[...]
    near = mm(halves(row), own[...])
    near = sea * (near[0:1] + near[1:2] - 6.0 * row)
    out[...] = base[...] + across(depth[...], cells) * row + across(rate[...], cells) * near


def finish_kernel(halo, swapped, closing, before, after, edge, part, speed, rate, out):
    levels, cells = part.shape
    first = before.shape[0] - 96
    rows = slice(first, first + 32)
    low = iota((32, LANES), 1) < TILE
    outer = jnp.where(low, before[rows, :].astype(F32), after[rows, :].astype(F32))[:levels]
    outer = jnp.where(in_group((levels, LANES)), outer, swapped[...] + closing[...]) * speed[...]
    pad = jnp.zeros((32 - levels, LANES), F32)
    outer = parts(jnp.concatenate([outer, pad], axis=0), 2)
    inner = halves(jnp.where(in_group((1, LANES)), halo[...], 0.0))
    near = mm(jnp.concatenate([outer, inner], axis=0), edge[...])
    inner = near[64:65] + near[65:66]
    out[...] = part[...] + (near[:32] + near[32:64])[:levels] + across(rate[...], cells) * inner


def call(kernel, out_shape, in_specs, out_specs, scratch=(), flops=2_000_000_000, vmem=24 * 2**20):
    return pl.pallas_call(
        kernel,
        out_shape=out_shape,
        in_specs=in_specs,
        out_specs=out_specs,
        scratch_shapes=list(scratch),
        cost_estimate=pl.CostEstimate(flops=flops, bytes_accessed=30_000_000, transcendentals=0),
        compiler_params=pltpu.CompilerParams(vmem_limit_bytes=vmem),
    )


def in_hbm(array):
    return pltpu.with_memory_space_constraint(array, pltpu.HBM)


def shards(
    ocean_fields,
    ocean_mask,
    entry_src,
    entry_route,
    entry_tile,
    weight_tiles,
    atm_state,
    atm_frac,
    couple,
    heat_coef,
    kappa,
    tracer,
    neighbours,
):
    fields, cells = ocean_fields.shape
    entries = entry_src.shape[0]
    atm_cells = atm_state.shape[1]
    rows = couple.shape[0]
    levels = tracer.shape[0]
    peers = lax.axis_size("blk")
    shape = jax.ShapeDtypeStruct
    half = rows // 2
    mask = ocean_mask.reshape(cells // LANES, LANES)
    route = entry_route.reshape(entries)
    pitch = 2 * (half + 1)
    i32 = jnp.int32
    sent = call(
        pack_kernel,
        shape((peers * pitch, LANES), BF16),
        [HBM] * 7,
        VMEM,
        [
            pltpu.SMEM((entries,), i32),
            pltpu.SMEM((entries,), i32),
            pltpu.SMEM((entries,), i32),
            pltpu.VMEM((fields, cells), BF16),
            pltpu.VMEM((cells // LANES, LANES), i32),
            pltpu.VMEM((rows, fields), F32),
            pltpu.VMEM((entries, TILE * TILE), BF16),
            pltpu.VMEM((cells // TILE, 4 * rows, TILE // 2), BF16),
            pltpu.VMEM(((entries + 1) * PITCH, LANES), F32),
            pltpu.VMEM((peers * pitch + 8, LANES), F32),
            pltpu.SMEM((peers,), i32),
            pltpu.SemaphoreType.DMA((7,)),
        ],
        vmem=64 * 2**20,
    )(entry_src, route, entry_tile, ocean_fields, mask, couple, weight_tiles)
    sent, weight_tiles, neighbours, atm_state, tracer = lax.optimization_barrier(
        (sent, weight_tiles, neighbours, atm_state, tracer)
    )
    got = lax.all_to_all(
        sent.reshape(peers, half + 1, 2, LANES), "blk", split_axis=0, concat_axis=0, tiled=True
    ).reshape(peers * pitch, LANES)
    here = call(
        ship_kernel,
        shape((entries * TILE // 2 + 96, LANES), BF16),
        [SMEM, SMEM, VMEM, VMEM, VMEM],
        VMEM,
        [pltpu.SMEM((peers,), i32), pltpu.VMEM(((entries + 1) * WIDE, LANES), F32)],
    )(*(in_hbm(x) for x in (entry_src, route, weight_tiles, tracer, mask)))
    axes = ("grp", "blk")
    count = lax.axis_size(axes)
    up = [(i, i - i % peers + (i + 1) % peers) for i in range(count)]
    down = [(target, source) for source, target in up]
    seams = [(i, (i + peers) % count) for i in range(0, count, peers)]
    seams += [(i, i - peers) for i in range(2 * peers - 1, count, peers)]
    before = lax.ppermute(here, axes, up)
    after = lax.ppermute(here, axes, down)
    mixed, shares, chosen = call(
        tables_kernel,
        (
            shape((16, half * LANES), F32),
            shape((16, LANES), F32),
            shape((16, entries * TILE), F32),
        ),
        [SMEM, VMEM, VMEM, VMEM],
        (VMEM,) * 3,
    )(entry_src, atm_state, atm_frac.reshape(atm_cells // LANES, LANES), couple)
    fluxes, back = call(
        merge_kernel,
        (shape((16, half * LANES), F32), shape((peers * 4, LANES), BF16)),
        [SMEM, VMEM, VMEM, VMEM],
        (VMEM, VMEM),
        [pltpu.VMEM((peers * pitch + 16, LANES), F32)],
    )(heat_coef, got, mixed, shares)
    back, neighbours, tracer = lax.optimization_barrier((back, neighbours, tracer))
    returned = lax.all_to_all(
        back.reshape(peers, 2, 2, LANES), "blk", split_axis=0, concat_axis=0, tiled=True
    ).reshape(peers * 4, LANES)
    own, edge, base, depth, speed, rate = call(
        base_kernel,
        (
            shape((cells, cells), BF16),
            shape((2 * HALO, cells), BF16),
            shape((levels, cells), F32),
            shape((levels, LANES), F32),
            shape((levels, LANES), F32),
            shape((levels, LANES), F32),
        ),
        [SMEM, VMEM, VMEM, VMEM],
        (VMEM,) * 6,
        flops=1_000_000_000,
    )(kappa, neighbours, tracer, mask)
    heat, forced, ends, halo = call(
        heat_kernel,
        (
            shape((1, cells), F32),
            shape((levels, LANES), F32),
            shape((levels, LANES), F32),
            shape((1, LANES), F32),
        ),
        [VMEM] * 7,
        (VMEM,) * 4,
        [pltpu.VMEM((peers * 4 + 8, LANES), F32)],
    )(returned, chosen, here, before, after, mask, depth)
    swapped = lax.ppermute(forced, axes, seams)
    closing = lax.ppermute(ends, axes, [(0, count - 1)])
    part, fluxes = call(
        partial_kernel,
        (shape((levels, cells), F32), shape((rows, atm_cells), BF16)),
        [VMEM] * 7,
        (VMEM, VMEM),
        flops=100_000_000,
    )(heat, own, base, mask, depth, rate, fluxes)
    tracer_out = call(finish_kernel, shape((levels, cells), F32), [VMEM] * 9, VMEM)(
        halo, swapped, closing, before, after, edge, part, speed, rate
    )
    return (fluxes, tracer_out)


def solution(mesh):
    split = ("grp", "blk")
    return jax.shard_map(
        shards,
        mesh=mesh,
        in_specs=(
            P(None, split),
            P(split),
            P(split),
            P(split, None),
            P(split),
            P(split, None),
            P(None, split),
            P(split),
            P(),
            P(),
            P(),
            P(None, split),
            P(None, split),
        ),
        out_specs=(P(None, split), P(None, split)),
        check_vma=False,
    )
```
